256 devices in a mesh: ctx: 64 (over z, x, core), head: 4 (over y).
Axes of the slice: x: 4, y: 4, z: 8, core: 2. Of those that a mesh axis runs over, the one named last changes fastest.
Arguments:
- activations: bfloat16 [8192, 8192], P('ctx', 'head'), may hold values from -6 to 6
- adapter_down: bfloat16 [8192, 768], P('head'), may hold values from -0.0625 to 0.0625
- adapter_ids: int32 [8192, 2], P('ctx'), may hold values from 0 to 7, all different within a row
- adapter_weight: float32 [8192, 2], P('ctx'), may hold values from 0.05 to 0.95, as said below
- query_base: bfloat16 [8192, 8192], P('ctx', 'head'), may hold values from -110 to 110
- key_base: bfloat16 [8192, 1024], P('ctx', 'head'), may hold values from -6 to 6
- value_base: bfloat16 [8192, 1024], P('ctx', 'head'), may hold values from -6 to 6
- up_query: bfloat16 [256, 8192], P(None, 'head'), may hold values from -1 to 1
- up_key: bfloat16 [256, 1024], P(None, 'head'), may hold values from -1 to 1
- up_value: bfloat16 [256, 1024], P(None, 'head'), may hold values from -1 to 1
Outputs:
- attended: bfloat16 [8192, 8192], P('ctx', 'head')
The draws below stay inside these ranges and needn't reach their ends.
Inputs may be any that keep to these rules, and one draw needn't show every extreme that they name: `adapter_weight`: each row holds two weights that sum to one, the first the larger.
All inputs are finite; a program needn't handle non-finite values.
Results may differ from the reference program's by a relative error of at most 0.029.
Values may be sent and summed in bfloat16 or wider, within the bound.
No kernel may reach another device: no remote copies, remote signals or barrier semaphores. Data moves between devices by JAX's collectives and lax.ppermute only.
A program may use at most 64 MiB of HBM per device.

```python
import math
import jax
import jax.numpy as jnp
from jax import lax

D = 8192
QH = 64
KVH = 8
HD = 128
ADAPTERS = 8
RANK = 32
TOKENS = 8192


def draw_adapter_weight(key, part):
    key = jax.random.fold_in(key, 5)
    leading = jax.random.uniform(key, (TOKENS, 1), jnp.float32, 0.5, 0.95)
    return jnp.concatenate([leading, 1.0 - leading], axis=1)


def draw_query_base(key, part):
    key = jax.random.fold_in(key, 11)
    shape_key = jax.random.fold_in(key, 0)
    values = jax.random.truncated_normal(shape_key, -6.0, 6.0, (TOKENS, QH * HD), jnp.float32)
    return values.astype(jnp.bfloat16)


def steps_of(stream_key, extent, cuts, smallest, high):
    loudness, own = 1.0, jax.random.fold_in(stream_key, 6)
    for position, shards_of in cuts:
        heights = jnp.exp(jax.random.uniform(jax.random.fold_in(own, position), (shards_of,), jnp.float32, smallest / len(cuts), high / len(cuts)))
        loudness = loudness * jnp.repeat(heights, extent[position] // shards_of).reshape([-1 if axis == position else 1 for axis in range(len(extent))])
    return loudness


def different_ones(stream_key, rows, amount, top, lift):
    order = jax.random.permutation(jax.random.fold_in(stream_key, 1), amount)
    pull = order
    for power in range(3):
        pull = pull * pull // amount
    pull = pull * lift // amount
    tickets = jax.random.randint(jax.random.fold_in(stream_key, 2), (rows, amount), 0, 4096) + pull
    fixed_rows = jax.random.permutation(jax.random.fold_in(stream_key, 3), rows)[jnp.arange(amount) % rows]
    tickets = jnp.where(jnp.arange(rows)[:, None] == fixed_rows[None, :], 1 << 14, tickets)
    priority = tickets * amount + jnp.arange(amount)
    return lax.top_k(priority.astype(jnp.int32), top)[1].astype(jnp.int32)


def centred(stream_key, extent, width, bound, shards=(), held_as=jnp.bfloat16):
    result = jax.random.normal(stream_key, extent, jnp.float32) * width
    if len(shards) > 0:
        result = steps_of(stream_key, extent, shards, -0.22, 0.18) * result
    return jnp.clip(result, min=-bound, max=bound).astype(held_as)


def setup_inputs(seed: int = 0) -> dict:
    seeds = jax.random.split(jax.random.key(seed), 11)
    activations = centred(seeds[0], (TOKENS, D), 1.0, 6.0, ((0, 64), (1, 4)))
    adapter_down = centred(seeds[1], (D, 3 * ADAPTERS * RANK), D ** -0.5, 0.0625, ((0, 4),))
    adapter_ids = different_ones(seeds[2], TOKENS, ADAPTERS, 2, 4096)
    adapter_weight = draw_adapter_weight(jax.random.fold_in(seeds[10], 71), 0)
    query_base = draw_query_base(jax.random.fold_in(seeds[10], 71), 0)
    key_base = centred(seeds[5], (TOKENS, KVH * HD), 1.0, 6.0, ((0, 64), (1, 4)))
    value_base = centred(seeds[6], (TOKENS, KVH * HD), 1.0, 6.0, ((0, 64), (1, 4)))
    up_query = centred(seeds[7], (ADAPTERS * RANK, QH * HD), RANK ** -0.5, 1.0, ((1, 4),))
    up_key = centred(seeds[8], (ADAPTERS * RANK, KVH * HD), RANK ** -0.5, 1.0, ((1, 4),))
    up_value = centred(seeds[9], (ADAPTERS * RANK, KVH * HD), RANK ** -0.5, 1.0, ((1, 4),))
    return dict(activations=activations, adapter_down=adapter_down, adapter_ids=adapter_ids, adapter_weight=adapter_weight, query_base=query_base, key_base=key_base, value_base=value_base, up_query=up_query, up_key=up_key, up_value=up_value)


rope_base = 500000.0
floor_value = -1e+30

def rotate(values, positions):
    row_count = values.shape[0]
    heads = values.shape[1] // HD
    half_width = HD // 2
    inverse = jnp.exp(jnp.arange(half_width, dtype=jnp.float32) * (-2.0 * math.log(rope_base) / HD))
    angles = positions.astype(jnp.float32)[:, None] * inverse[None, :]
    cosine = jnp.cos(angles)[:, None, :]
    sine = jnp.sin(angles)[:, None, :]
    shaped = values.reshape(row_count, heads, HD)
    first_half = shaped[:, :, :half_width]
    second_half = shaped[:, :, half_width:]
    turned = jnp.concatenate([first_half * cosine - second_half * sine, second_half * cosine + first_half * sine], axis=2)
    return turned.reshape(row_count, heads * HD)

def mixture(adapter_ids, adapter_weight):
    labels = jnp.arange(ADAPTERS, dtype=jnp.int32)
    matches = (adapter_ids[:, :, None] == labels[None, None, :]).astype(jnp.float32)
    return lax.optimization_barrier(jnp.sum(matches * adapter_weight[:, :, None], axis=1))

def gate_rows(low_rank, coefficient):
    row_count = low_rank.shape[0]
    shaped = low_rank.reshape(row_count, 3, ADAPTERS, RANK)
    gated = shaped * coefficient[:, None, :, None]
    return gated.astype(jnp.bfloat16).reshape(row_count, 3 * ADAPTERS * RANK)

def project(gated, query_base, key_base, value_base, up_query, up_key, up_value, positions):
    span = ADAPTERS * RANK
    query_raw = query_base.astype(jnp.float32) + jnp.dot(gated[:, :span], up_query, preferred_element_type=jnp.float32)
    key_raw = key_base.astype(jnp.float32) + jnp.dot(gated[:, span:2 * span], up_key, preferred_element_type=jnp.float32)
    value_raw = value_base.astype(jnp.float32) + jnp.dot(gated[:, 2 * span:], up_value, preferred_element_type=jnp.float32)
    query = rotate(query_raw, positions).astype(jnp.bfloat16)
    keys = rotate(key_raw, positions).astype(jnp.bfloat16)
    return (query, keys, value_raw.astype(jnp.bfloat16))

def reference(activations, adapter_down, adapter_ids, adapter_weight, query_base, key_base, value_base, up_query, up_key, up_value):
    low_rank = jnp.dot(activations, adapter_down, preferred_element_type=jnp.float32)
    gated = gate_rows(low_rank, mixture(adapter_ids, adapter_weight))
    positions = jnp.arange(TOKENS, dtype=jnp.int32)
    query, keys, values = project(gated, query_base, key_base, value_base, up_query, up_key, up_value, positions)
    group_size = QH // KVH
    scale_factor = 1.0 / math.sqrt(HD)
    query_wide = lax.optimization_barrier(query).astype(jnp.float32).reshape(TOKENS, KVH, group_size, HD).transpose(1, 2, 0, 3)
    key_wide = lax.optimization_barrier(keys).astype(jnp.float32).reshape(TOKENS, KVH, HD).transpose(1, 0, 2)
    value_wide = lax.optimization_barrier(values).astype(jnp.float32).reshape(TOKENS, KVH, HD).transpose(1, 0, 2)
    block_rows = math.gcd(TOKENS, 512)
    block_count = TOKENS // block_rows

    def per_head(operands):
        query_head, key_head, value_head = operands

        def per_block(block_start):
            query_block = lax.dynamic_slice_in_dim(query_head, block_start, block_rows, 1)
            query_pos = block_start + jnp.arange(block_rows, dtype=jnp.int32)
            scores = jnp.einsum('gqd,kd->gqk', query_block, key_head, precision=lax.Precision.HIGHEST) * scale_factor
            allowed = (query_pos[:, None] >= positions[None, :])[None]
            scores = jnp.where(allowed, scores, floor_value)
            top_score = lax.optimization_barrier(jnp.max(scores, axis=2, keepdims=True))
            expo = jnp.where(allowed, jnp.exp(scores - top_score), 0.0)
            total = lax.optimization_barrier(jnp.sum(expo, axis=2, keepdims=True))
            rounded = lax.optimization_barrier(expo.astype(jnp.bfloat16)).astype(jnp.float32)
            summed = jnp.einsum('gqk,kd->gqd', rounded, value_head, precision=lax.Precision.HIGHEST)
            return (summed / total).astype(jnp.bfloat16)
        starts = jnp.arange(block_count, dtype=jnp.int32) * block_rows
        return lax.map(per_block, starts)
    outputs = lax.map(per_head, (query_wide, key_wide, value_wide))
    return outputs.transpose(1, 3, 0, 2, 4).reshape(TOKENS, QH * HD)
```

```python
import functools
import math

import jax
import jax.numpy as jnp
from jax import lax
from jax.experimental import pallas as pl
from jax.experimental.pallas import tpu as pltpu
from jax.sharding import PartitionSpec as P

HD = 128
ADAPTERS = 8
RANK = 32
SPAN = ADAPTERS * RANK
ROWS = 128
GROUP = 8
ZS, XS, YS = 8, 4, 4
BLOCK = 2 * ROWS
SLAB = XS * BLOCK

rope_base = 500000.0
floor_value = -1e30
FACTOR = math.log2(math.e) / math.sqrt(HD)
VMEM_LIMIT = 40 * 1024 * 1024


def device(z, x, core, y):
    return (((z % ZS) * XS + x % XS) * 2 + core) * YS + y


def send(array, move):
    pairs = []
    for z in range(ZS):
        for x in range(XS):
            for core in range(2):
                for y in range(YS):
                    pairs.append((device(z, x, core, y), device(*move(z, x, core, y))))
    return lax.ppermute(array, ("ctx", "head"), pairs)


def swap_cores(array):
    return send(array, lambda z, x, core, y: (z, x, 1 - core, y))


def turn(raw, cosine, sine):
    return raw * cosine + pltpu.roll(raw, HD // 2, 1) * sine


def kv_kernel(core_ref, low_ref, more_ref, coef_ref, upk_ref, upv_ref, kb_ref, vb_ref, cos_ref, sin_ref, kv_ref, gq_ref):
    core = core_ref[0]
    coef = coef_ref[...]

    def gated(part):
        cols = slice(part * SPAN, (part + 1) * SPAN)
        return ((low_ref[:, cols] + more_ref[:, cols]) * coef).astype(jnp.bfloat16)

    gq_ref[...] = gated(0)
    key_raw = kb_ref[...].astype(jnp.float32) + jnp.dot(gated(1), upk_ref[...], preferred_element_type=jnp.float32)
    value = vb_ref[...].astype(jnp.float32) + jnp.dot(gated(2), upv_ref[...], preferred_element_type=jnp.float32)
    cosine, sine = cos_ref[...], sin_ref[...]
    keys = [turn(key_raw[:, h * HD : (h + 1) * HD], cosine, sine) for h in range(2)]
    values = [value[:, h * HD : (h + 1) * HD] for h in range(2)]
    first = core == 0
    kv_ref[0, :, :HD] = jnp.where(first, keys[0], keys[1]).astype(jnp.bfloat16)
    kv_ref[1, :, :HD] = jnp.where(first, keys[1], keys[0]).astype(jnp.bfloat16)
    kv_ref[0, :, HD:] = jnp.where(first, values[0], values[1]).astype(jnp.bfloat16)
    kv_ref[1, :, HD:] = jnp.where(first, values[1], values[0]).astype(jnp.bfloat16)


def q_kernel(core_ref, gq_ref, upq_ref, qb_ref, cos_ref, sin_ref, mine_ref, other_ref):
    core = core_ref[0]
    cosine, sine = cos_ref[...], sin_ref[...]
    gq = gq_ref[...]
    for target, group in ((other_ref, 1 - core), (mine_ref, core)):
        for j in range(GROUP):
            cols = pl.ds(pl.multiple_of((group * GROUP + j) * HD, HD), HD)
            raw = qb_ref[:, cols].astype(jnp.float32) + jnp.dot(
                gq, upq_ref[:, cols], preferred_element_type=jnp.float32
            )
            target[:, j * HD : (j + 1) * HD] = turn(raw, cosine, sine).astype(jnp.bfloat16)


def query_tile(qo_ref, qr_ref, g):
    cols = pl.ds(pl.multiple_of(g * HD, HD), HD)
    return jnp.concatenate([qo_ref[:, cols], qr_ref[:, cols]], axis=0)


def scores_of(query, keys):
    return lax.dot_general(query, keys, (((1,), (1,)), ((), ())), preferred_element_type=jnp.float32)


def pieces(array):
    return [array[:, j * HD : (j + 1) * HD] for j in range(array.shape[1] // HD)]


def weigh(parts, top, values):
    expo = [jnp.exp2(part * FACTOR - top) for part in parts]
    total = functools.reduce(jnp.add, expo)
    weights = jnp.concatenate([e.astype(jnp.bfloat16) for e in expo], axis=1)
    return total, jnp.dot(weights, values, preferred_element_type=jnp.float32)


def first_kernel(base_ref, qo_ref, qr_ref, kv_ref, top_ref, total_ref, acc_ref):
    row = lax.broadcasted_iota(jnp.int32, (ROWS, HD), 0)
    lane = lax.broadcasted_iota(jnp.int32, (ROWS, HD), 1)
    gap = jnp.concatenate([row - lane + base_ref[8], row - lane + base_ref[9]], axis=0)

    def body(g, carry):
        query = query_tile(qo_ref, qr_ref, g)
        scores = scores_of(query, kv_ref[0, :, :HD])
        parts = [
            jnp.where(gap >= base_ref[j], part, floor_value) for j, part in enumerate(pieces(scores))
        ]
        best = jnp.max(functools.reduce(jnp.maximum, parts), axis=1, keepdims=True)
        top = jnp.broadcast_to(best * FACTOR, (BLOCK, HD))
        total, acc = weigh(parts, top, kv_ref[0, :, HD:])
        top_ref[g] = top
        total_ref[g] = total
        acc_ref[g] = acc
        return carry

    lax.fori_loop(0, GROUP, body, 0)


def update(qo_ref, qr_ref, keys, values, top_ref, total_ref, acc_ref, g):
    query = query_tile(qo_ref, qr_ref, g)
    parts = pieces(scores_of(query, keys))
    best = jnp.max(functools.reduce(jnp.maximum, parts), axis=1, keepdims=True)
    old = top_ref[g]
    top = jnp.maximum(old, best * FACTOR)
    shrink = jnp.exp2(old - top)
    total, acc = weigh(parts, top, values)
    top_ref[g] = top
    total_ref[g] = total_ref[g] * shrink + total
    acc_ref[g] = acc_ref[g] * shrink + acc


def next_kernel(flag_ref, qo_ref, qr_ref, near_ref, far_ref, top_in, total_in, acc_in, top_ref, total_ref, acc_ref):
    top_ref[...] = top_in[...]
    total_ref[...] = total_in[...]
    acc_ref[...] = acc_in[...]
    for index, kv in enumerate((near_ref, far_ref)):

        @pl.when(flag_ref[index] != 0)
        def _(kv=kv):
            def body(g, carry):
                keys, values = kv[0, :, :HD], kv[0, :, HD:]
                update(qo_ref, qr_ref, keys, values, top_ref, total_ref, acc_ref, g)
                return carry

            lax.fori_loop(0, GROUP, body, 0)


def last_kernel(flag_ref, qo_ref, qr_ref, near_ref, far_ref, top_in, total_in, acc_in, own_ref, other_ref, top_ref, total_ref, acc_ref):
    next_kernel(
        flag_ref, qo_ref, qr_ref, near_ref, far_ref, top_in, total_in, acc_in, top_ref, total_ref, acc_ref
    )
    for g in range(GROUP):
        total = jnp.sum(total_ref[g], axis=1, keepdims=True)
        out = (acc_ref[g] / total).astype(jnp.bfloat16)
        own_ref[:, g * HD : (g + 1) * HD] = out[:ROWS]
        other_ref[:, g * HD : (g + 1) * HD] = out[ROWS:]


def whole():
    return pl.BlockSpec(memory_space=pltpu.VMEM)


def scalars():
    return pl.BlockSpec(memory_space=pltpu.SMEM)


def call(kernel, n_in, outs, flops, scratch=()):
    return pl.pallas_call(
        kernel,
        out_shape=outs,
        in_specs=[scalars()] + [whole()] * n_in,
        out_specs=tuple(whole() for _ in outs),
        scratch_shapes=list(scratch),
        compiler_params=pltpu.CompilerParams(vmem_limit_bytes=VMEM_LIMIT),
        cost_estimate=pl.CostEstimate(flops=flops, bytes_accessed=4 << 20, transcendentals=0),
    )


def on_device(activations, adapter_down, adapter_ids, adapter_weight, query_base, key_base, value_base, up_query, up_key, up_value):
    ctx = lax.axis_index("ctx").astype(jnp.int32)
    z, x, core = ctx // (2 * XS), (ctx // 2) % XS, ctx % 2
    cores = core.reshape(1)
    f32, b16 = jnp.float32, jnp.bfloat16

    partial_low = jnp.dot(activations, adapter_down, preferred_element_type=f32)

    labels = jnp.arange(SPAN, dtype=jnp.int32) // RANK
    coef = jnp.zeros((ROWS, SPAN), f32)
    for j in range(adapter_ids.shape[1]):
        coef = coef + jnp.where(adapter_ids[:, j : j + 1] == labels[None, :], adapter_weight[:, j : j + 1], 0.0)
    positions = (ctx * ROWS + jnp.arange(ROWS, dtype=jnp.int32)).astype(f32)
    inverse = jnp.exp(jnp.arange(HD // 2, dtype=f32) * (-2.0 * math.log(rope_base) / HD))
    angles = positions[:, None] * jnp.concatenate([inverse, inverse])[None, :]
    cosine = jnp.cos(angles)
    sign = jnp.where(jnp.arange(HD) < HD // 2, -1.0, 1.0).astype(f32)
    sine = jnp.sin(angles) * sign[None, :]

    one = send(partial_low, lambda z, x, c, y: (z, x, c, y ^ (1 if c == 0 else 3)))
    low = partial_low + one
    two = send(low, lambda z, x, c, y: (z, x, c, y ^ (3 if c == 0 else 1)))

    kv, gated_query = call(
        kv_kernel,
        9,
        (jax.ShapeDtypeStruct((2, ROWS, 2 * HD), b16), jax.ShapeDtypeStruct((ROWS, SPAN), b16)),
        1 << 27,
    )(cores, low, two, coef, up_key, up_value, key_base, value_base, cosine, sine)

    got = send(kv, lambda z, x, c, y: (z, x ^ (1 if c == 0 else 3), c, y))
    pair = jnp.concatenate([kv, got], axis=1)
    far_pair = send(pair, lambda z, x, c, y: (z, x ^ (3 if c == 0 else 1), c, y))
    half = jnp.concatenate([pair, far_pair], axis=1)
    rest = swap_cores(half)
    slab = jnp.concatenate([half, rest[::-1]], axis=1)

    half_shape = jax.ShapeDtypeStruct((ROWS, GROUP * HD), b16)
    q_own, q_other = call(q_kernel, 5, (half_shape, half_shape), 1 << 29)(
        cores, gated_query, up_query, query_base, cosine, sine
    )
    q_rest = swap_cores(q_other)

    state_shape = (jax.ShapeDtypeStruct((GROUP, BLOCK, HD), f32),) * 3
    step_x = jnp.where(core == 0, 1, 3)
    own_x = jnp.stack([x, x ^ step_x, x ^ (4 - step_x), x ^ 2])
    rest_x = jnp.stack([x, x ^ (4 - step_x), x ^ step_x, x ^ 2])
    bases = jnp.concatenate(
        [
            (own_x - x) * BLOCK + core * ROWS,
            (rest_x - x) * BLOCK + (1 - core) * ROWS,
            jnp.stack([core * ROWS, (1 - core) * ROWS]),
        ]
    ).astype(jnp.int32)
    state = call(first_kernel, 3, state_shape, 1 << 32)(bases, q_own, q_rest, slab)

    moving = slab
    for step in range(1, 4):
        moving = send(moving, lambda z, x, c, y: (z + (1 if c == 0 else -1), x, c, y))
        swapped = swap_cores(moving[1:])
        below = (z >= step).astype(jnp.int32)
        wrapped = (z + step >= ZS).astype(jnp.int32)
        flags = jnp.where(core == 0, jnp.stack([below, wrapped]), jnp.stack([wrapped, below]))
        state = call(next_kernel, 7, state_shape, 1 << 33)(flags, q_own, q_rest, moving, swapped, *state)
    ends = send(moving[:, : SLAB // 2], lambda z, x, c, y: (z + (1 if c == 0 else -1), x, c, y))
    swapped = swap_cores(ends[1:])
    flags = jnp.stack([z >= ZS // 2, z >= ZS // 2]).astype(jnp.int32)
    own, other = call(
        last_kernel,
        7,
        (half_shape, half_shape),
        1 << 32,
        scratch=[pltpu.VMEM((GROUP, BLOCK, HD), f32)] * 3,
    )(flags, q_own, q_rest, ends, swapped, *state)
    back = swap_cores(other)
    return jnp.concatenate([jnp.where(core == 0, own, back), jnp.where(core == 0, back, own)], axis=1)


def solution(mesh):
    in_specs = (
        P("ctx", "head"),
        P("head", None),
        P("ctx", None),
        P("ctx", None),
        P("ctx", "head"),
        P("ctx", "head"),
        P("ctx", "head"),
        P(None, "head"),
        P(None, "head"),
        P(None, "head"),
    )
    return jax.shard_map(on_device, mesh=mesh, in_specs=in_specs, out_specs=P("ctx", "head"), check_vma=False)
```

```python
import math

import jax
import jax.numpy as jnp
from jax import lax
from jax.experimental import pallas as pl
from jax.experimental.pallas import tpu as pltpu
from jax.sharding import PartitionSpec as P

HD = 128
ADAPTERS = 8
RANK = 32
SPAN = ADAPTERS * RANK
ROWS = 128
GROUP = 8
ZS, XS, YS = 8, 4, 4
BLOCK = 2 * ROWS
SLAB = XS * BLOCK
SIDE = GROUP * ROWS

rope_base = 500000.0
floor_value = -1e30
FACTOR = math.log2(math.e) / math.sqrt(HD)
VMEM_LIMIT = 40 * 1024 * 1024


def device(z, x, core, y):
    return (((z % ZS) * XS + x % XS) * 2 + core) * YS + y


def send(array, move):
    pairs = []
    for z in range(ZS):
        for x in range(XS):
            for core in range(2):
                for y in range(YS):
                    pairs.append((device(z, x, core, y), device(*move(z, x, core, y))))
    return lax.ppermute(array, ("ctx", "head"), pairs)


def swap_cores(array):
    return send(array, lambda z, x, core, y: (z, x, 1 - core, y))


def turn(raw, cosine, sine):
    return raw * cosine + pltpu.roll(raw, HD // 2, 1) * sine


def low_kernel(act_hbm, down_hbm, low_ref, sent_ref, act_ref, down_ref, act_sem, down_sem):
    pieces = act_sem.shape[0]
    depth = act_ref.shape[1] // pieces
    copies = []
    for k in range(pieces):
        span = slice(k * depth, (k + 1) * depth)
        copies.append(
            (
                pltpu.make_async_copy(act_hbm.at[:, span], act_ref.at[:, span], act_sem.at[k]),
                pltpu.make_async_copy(down_hbm.at[span], down_ref.at[span], down_sem.at[k]),
            )
        )
        for copy in copies[-1]:
            copy.start()
    total = None
    for k in range(pieces):
        span = slice(k * depth, (k + 1) * depth)
        for copy in copies[k]:
            copy.wait()
        part = jnp.dot(act_ref[:, span], down_ref[span], preferred_element_type=jnp.float32)
        total = part if total is None else total + part
    low_ref[...] = total
    sent_ref[...] = total.astype(jnp.bfloat16)


def low_product(activations, adapter_down):
    rows, columns = activations.shape[0], adapter_down.shape[1]
    pieces = 8
    return pl.pallas_call(
        low_kernel,
        in_specs=[pl.BlockSpec(memory_space=pltpu.HBM)] * 2,
        out_specs=(whole(), whole()),
        out_shape=(
            jax.ShapeDtypeStruct((rows, columns), jnp.float32),
            jax.ShapeDtypeStruct((rows, columns), jnp.bfloat16),
        ),
        scratch_shapes=[
            pltpu.VMEM(activations.shape, activations.dtype),
            pltpu.VMEM(adapter_down.shape, adapter_down.dtype),
            pltpu.SemaphoreType.DMA((pieces,)),
            pltpu.SemaphoreType.DMA((pieces,)),
        ],
        compiler_params=pltpu.CompilerParams(vmem_limit_bytes=56 * 1024 * 1024),
        cost_estimate=pl.CostEstimate(flops=1 << 29, bytes_accessed=4 << 20, transcendentals=0),
    )(activations, adapter_down)


def kv_kernel(group_ref, low_ref, more_ref, coef_ref, upk_ref, upv_ref, kb_ref, vb_ref, cos_ref, sin_ref, mine_ref, other_ref, gq_ref):
    group = group_ref[0]
    coef = coef_ref[...]

    def gated(part):
        cols = slice(part * SPAN, (part + 1) * SPAN)
        return ((low_ref[:, cols] + more_ref[:, cols].astype(jnp.float32)) * coef).astype(jnp.bfloat16)

    gq_ref[...] = gated(0)
    key_raw = kb_ref[...].astype(jnp.float32) + jnp.dot(gated(1), upk_ref[...], preferred_element_type=jnp.float32)
    value = vb_ref[...].astype(jnp.float32) + jnp.dot(gated(2), upv_ref[...], preferred_element_type=jnp.float32)
    cosine, sine = cos_ref[...], sin_ref[...]
    keys = [turn(key_raw[:, h * HD : (h + 1) * HD], cosine, sine) for h in range(2)]
    values = [value[:, h * HD : (h + 1) * HD] for h in range(2)]
    first = group == 0
    mine_ref[:, :HD] = jnp.where(first, keys[0], keys[1]).astype(jnp.bfloat16)
    mine_ref[:, HD:] = jnp.where(first, values[0], values[1]).astype(jnp.bfloat16)
    other_ref[:, :HD] = jnp.where(first, keys[1], keys[0]).astype(jnp.bfloat16)
    other_ref[:, HD:] = jnp.where(first, values[1], values[0]).astype(jnp.bfloat16)


def q_kernel(group_ref, gq_ref, upq_ref, qb_ref, cos_ref, sin_ref, mine_ref, *other_refs):
    own = group_ref[0]
    cosine, sine = cos_ref[...], sin_ref[...]
    gq = gq_ref[...]
    start = (1 - own) * GROUP
    for target in (*other_refs, mine_ref):
        heads = target.shape[1] // HD
        if target is mine_ref:
            start = own * GROUP
        for j in range(heads):
            cols = pl.ds(pl.multiple_of((start + j) * HD, HD), HD)
            raw = qb_ref[:, cols].astype(jnp.float32) + jnp.dot(
                gq, upq_ref[:, cols], preferred_element_type=jnp.float32
            )
            target[:, j * HD : (j + 1) * HD] = turn(raw, cosine, sine).astype(jnp.bfloat16)
        start = start + heads


def pair_kernel(a_ref, b_ref, out_ref):
    rows = a_ref.shape[0]
    out_ref[:rows] = a_ref[...]
    out_ref[rows:] = b_ref[...]


def queries(refs):
    tiles = [ref[:, g * HD : (g + 1) * HD] for ref in refs for g in range(ref.shape[1] // HD)]
    return jnp.concatenate(tiles, axis=0)


def scores_of(keys, query):
    return lax.dot_general(keys, query, (((1,), (1,)), ((), ())), preferred_element_type=jnp.float32)


def weighted(values, weights):
    return lax.dot_general(values, weights, (((0,), (0,)), ((), ())), preferred_element_type=jnp.float32)


def first_kernel(base_ref, *refs):
    *q_refs, a_ref, b_ref, top_ref, total_ref, acc_ref = refs
    kv = jnp.concatenate([a_ref[...], b_ref[...]], axis=0)
    scores = scores_of(kv[:, :HD], queries(q_refs))
    gap = lax.broadcasted_iota(jnp.int32, (ROWS, HD), 1) - lax.broadcasted_iota(jnp.int32, (ROWS, HD), 0)
    lines = []
    for j in range(SLAB // ROWS):
        rows = slice(j * ROWS, (j + 1) * ROWS)
        allowed = gap >= base_ref[j] - base_ref[SLAB // ROWS]
        parts = [jnp.where(allowed, scores[rows, g * HD : (g + 1) * HD], floor_value) for g in range(GROUP)]
        lines.append(jnp.concatenate(parts, axis=1))
    scores = jnp.concatenate(lines, axis=0).reshape(SLAB // 8, 8, SIDE)
    top = jnp.max(jnp.max(scores, axis=0), axis=0, keepdims=True) * FACTOR
    top = jnp.broadcast_to(top, (8, SIDE))
    expo = jnp.exp2(scores * FACTOR - top[None])
    top_ref[...] = top
    total_ref[...] = jnp.sum(expo, axis=0)
    acc_ref[...] = weighted(kv[:, HD:], expo.astype(jnp.bfloat16).reshape(SLAB, SIDE))


def step_of(query, kv, old):
    keys, cols = kv.shape[0], query.shape[0]
    scores = scores_of(kv[:, :HD], query).reshape(keys // 8, 8, cols)
    best = jnp.max(jnp.max(scores, axis=0), axis=0, keepdims=True)
    top = jnp.maximum(old, best * FACTOR)
    expo = jnp.exp2(scores * FACTOR - top[None])
    shrink = jnp.exp2(old - top)
    acc = weighted(kv[:, HD:], expo.astype(jnp.bfloat16).reshape(keys, cols))
    return top, shrink, jnp.sum(expo, axis=0), acc


def next_kernel(flag_ref, *refs):
    q_refs, (a_ref, b_ref), ins, outs = refs[:3], refs[3:5], refs[5:11], refs[11:]

    @pl.when(flag_ref[0] != 0)
    def _():
        kv = jnp.concatenate([a_ref[...], b_ref[...]], axis=0)
        old = jnp.concatenate([ins[0][...], ins[3][...]], axis=1)
        top, shrink, total, acc = step_of(queries(q_refs), kv, old)
        for side in range(2):
            cols = slice(side * SIDE, (side + 1) * SIDE)
            outs[3 * side][...] = top[:, cols]
            outs[3 * side + 1][...] = ins[3 * side + 1][...] * shrink[:, cols] + total[:, cols]
            outs[3 * side + 2][...] = ins[3 * side + 2][...] * shrink[:1, cols] + acc[:, cols]


def last_kernel(flag_ref, *refs):
    *q_refs, a_ref, b_ref, top_ref, total_ref, acc_ref, out_ref, last_total, last_acc = refs
    last_total[...] = total_ref[...]
    last_acc[...] = acc_ref[...]

    @pl.when(flag_ref[0] != 0)
    def _():
        kv = jnp.concatenate([a_ref[...], b_ref[...]], axis=0)
        unused, shrink, total, acc = step_of(queries(q_refs), kv, top_ref[...])
        last_total[...] = total_ref[...] * shrink + total
        last_acc[...] = acc_ref[...] * shrink[:1] + acc

    scale = 1.0 / jnp.sum(last_total[...], axis=0, keepdims=True)
    for g in range(GROUP):
        cols = slice(g * HD, (g + 1) * HD)
        out_ref[:, cols] = (last_acc[:, cols] * scale[:, cols]).T.astype(jnp.bfloat16)


def whole():
    return pl.BlockSpec(memory_space=pltpu.VMEM)


def call(kernel, n_in, outs, flops, n_scalar=1, aliases=None, scratch=()):
    return pl.pallas_call(
        kernel,
        out_shape=outs,
        in_specs=[pl.BlockSpec(memory_space=pltpu.SMEM)] * n_scalar + [whole()] * n_in,
        out_specs=tuple(whole() for _ in outs),
        input_output_aliases=aliases or {},
        scratch_shapes=list(scratch),
        compiler_params=pltpu.CompilerParams(vmem_limit_bytes=VMEM_LIMIT),
        cost_estimate=pl.CostEstimate(flops=flops, bytes_accessed=4 << 20, transcendentals=0),
    )


def after(array, *others):
    return lax.optimization_barrier((array,) + others)


def on_device(activations, adapter_down, adapter_ids, adapter_weight, query_base, key_base, value_base, up_query, up_key, up_value):
    ctx = lax.axis_index("ctx").astype(jnp.int32)
    z, x, core = ctx // (2 * XS), (ctx // 2) % XS, ctx % 2
    group = ((x + 1) // 2) % 2
    groups = group.reshape(1)
    f32, b16 = jnp.float32, jnp.bfloat16
    shape = jax.ShapeDtypeStruct

    partial_low, sent = low_product(activations, adapter_down)
    one = send(sent, lambda z, x, c, y: (z, x, c, y ^ (1 if c == 0 else 3)))

    labels = jnp.arange(SPAN, dtype=jnp.int32) // RANK
    coef = jnp.zeros((ROWS, SPAN), f32)
    for j in range(adapter_ids.shape[1]):
        coef = coef + jnp.where(adapter_ids[:, j : j + 1] == labels[None, :], adapter_weight[:, j : j + 1], 0.0)
    positions = (ctx * ROWS + jnp.arange(ROWS, dtype=jnp.int32)).astype(f32)
    inverse = jnp.exp(jnp.arange(HD // 2, dtype=f32) * (-2.0 * math.log(rope_base) / HD))
    angles = positions[:, None] * jnp.concatenate([inverse, inverse])[None, :]
    cosine = jnp.cos(angles)
    sign = jnp.where(jnp.arange(HD) < HD // 2, -1.0, 1.0).astype(f32)
    sine = jnp.sin(angles) * sign[None, :]
    one, coef, cosine, sine = after(one, coef, cosine, sine)

    low = partial_low + one.astype(f32)
    two = send(low.astype(b16), lambda z, x, c, y: (z, x, c, y ^ (3 if c == 0 else 1)))

    kv_shape = shape((ROWS, 2 * HD), b16)
    kv, kv_other, gated_query = call(kv_kernel, 9, (kv_shape, kv_shape, shape((ROWS, SPAN), b16)), 1 << 27)(
        groups, low, two, coef, up_key, up_value, key_base, value_base, cosine, sine
    )

    def neighbour(array):
        return send(array, lambda z, x, c, y: (z, x ^ 1, c, y))

    got = neighbour(kv_other)
    side_shape = shape((ROWS, GROUP * HD), b16)
    piece_shape = shape((ROWS, GROUP * HD // 2), b16)
    q_own, *q_other = call(q_kernel, 5, (side_shape, piece_shape, piece_shape), 1 << 29)(
        groups, gated_query, up_query, query_base, cosine, sine
    )
    got, q_own, *q_other = after(got, q_own, *q_other)
    pair = call(pair_kernel, 2, (shape((2 * ROWS, 2 * HD), b16),), 1 << 20, 0)(kv, got)[0]
    far = send(pair, lambda z, x, c, y: (z, x ^ 3, c, y))
    q_rest = [neighbour(piece) for piece in q_other]
    far, q_rest[0] = after(far, q_rest[0])
    moving_a = call(pair_kernel, 2, (shape((SLAB // 2, 2 * HD), b16),), 1 << 20, 0)(pair, far)[0]

    def ring(array):
        return send(array, lambda z, x, c, y: (z + (1 if c == 0 else -1), x, c, y))

    arriving_a = ring(moving_a)
    moving_b = swap_cores(moving_a)
    arriving_b = ring(moving_b)

    blocks = (jnp.stack([x, x ^ 1, x ^ 3, x ^ 2]) - x) * BLOCK
    keys_at = jnp.concatenate([blocks + core * ROWS, blocks + (1 - core) * ROWS])

    def bases(start):
        return jnp.concatenate([keys_at, start.reshape(1)]).astype(jnp.int32)

    state_shape = (shape((8, SIDE), f32), shape((8, SIDE), f32), shape((HD, SIDE), f32))
    state = [
        *call(first_kernel, 3, state_shape, 1 << 31)(bases(core * ROWS), q_own, moving_a, moving_b),
    ]
    state += call(first_kernel, 4, state_shape, 1 << 31)(
        bases(((x ^ 1) - x) * BLOCK + core * ROWS), *q_rest, moving_a, moving_b
    )

    def attend(flag, a, b, state):
        return call(next_kernel, 11, state_shape * 2, 1 << 32, 1, {6 + k: k for k in range(6)})(
            flag.astype(jnp.int32).reshape(1), q_own, *q_rest, a, b, *state
        )

    for step in range(1, 4):
        below, wrapped = z >= step, z + step >= ZS
        moving_a, *state = after(arriving_a, *state)
        arriving_a = ring(moving_a)
        swapped_a = swap_cores(moving_a)
        moving_b = arriving_b
        arriving_b = ring(moving_b)
        swapped_b = swap_cores(moving_b)
        state = attend(jnp.where(core == 0, below, wrapped), moving_a, moving_b, state)
        state = attend(jnp.where(core == 0, wrapped, below), swapped_a, swapped_b, state)
    moving_a, moving_b, *state = after(arriving_a, arriving_b, *state)
    flag = (z >= ZS // 2).astype(jnp.int32).reshape(1)

    def finish(query, state):
        scratch = [pltpu.VMEM((8, SIDE), f32), pltpu.VMEM((HD, SIDE), f32)]
        return call(last_kernel, len(query) + 5, (side_shape,), 1 << 31, scratch=scratch)(
            flag, *query, moving_a, moving_b, *state
        )[0]

    back = neighbour(finish(q_rest, state[3:]))
    own = finish([q_own], state[:3])
    return jnp.concatenate([jnp.where(group == 0, own, back), jnp.where(group == 0, back, own)], axis=1)


def solution(mesh):
    in_specs = (
        P("ctx", "head"),
        P("head", None),
        P("ctx", None),
        P("ctx", None),
        P("ctx", "head"),
        P("ctx", "head"),
        P("ctx", "head"),
        P(None, "head"),
        P(None, "head"),
        P(None, "head"),
    )
    return jax.shard_map(on_device, mesh=mesh, in_specs=in_specs, out_specs=P("ctx", "head"), check_vma=False)
```

```python
import functools
import math

import jax
import jax.numpy as jnp
from jax import lax
from jax.experimental import pallas as pl
from jax.experimental.pallas import tpu as pltpu
from jax.sharding import PartitionSpec as P

HD = 128
ADAPTERS = 8
RANK = 32
SPAN = ADAPTERS * RANK
ROWS = 128
GROUP = 8
ZS, XS, YS = 8, 4, 4
BLOCK = 2 * ROWS
SLAB = XS * BLOCK
SIDE = GROUP * ROWS

rope_base = 500000.0
floor_value = -1e30
FACTOR = math.log2(math.e) / math.sqrt(HD)
ROOM = 2.0**60
VMEM_LIMIT = 40 * 1024 * 1024


def device(z, x, core, y):
    return (((z % ZS) * XS + x % XS) * 2 + core) * YS + y


def send(array, move):
    pairs = []
    for z in range(ZS):
        for x in range(XS):
            for core in range(2):
                for y in range(YS):
                    pairs.append((device(z, x, core, y), device(*move(z, x, core, y))))
    return lax.ppermute(array, ("ctx", "head"), pairs)


def swap_cores(array):
    return send(array, lambda z, x, core, y: (z, x, 1 - core, y))


def turn(raw, cosine, sine):
    return raw * cosine + pltpu.roll(raw, HD // 2, 1) * sine


def low_kernel(act_hbm, down_hbm, low_ref, sent_ref, act_ref, down_ref, act_sem, down_sem):
    pieces = act_sem.shape[0]
    depth = act_ref.shape[1] // pieces
    copies = []
    for k in range(pieces):
        span = slice(k * depth, (k + 1) * depth)
        copies.append(
            (
                pltpu.make_async_copy(act_hbm.at[:, span], act_ref.at[:, span], act_sem.at[k]),
                pltpu.make_async_copy(down_hbm.at[span], down_ref.at[span], down_sem.at[k]),
            )
        )
        for copy in copies[-1]:
            copy.start()
    total = None
    for k in range(pieces):
        span = slice(k * depth, (k + 1) * depth)
        for copy in copies[k]:
            copy.wait()
        part = jnp.dot(act_ref[:, span], down_ref[span], preferred_element_type=jnp.float32)
        total = part if total is None else total + part
    low_ref[...] = total
    sent_ref[...] = total.astype(jnp.bfloat16)


def low_product(activations, adapter_down):
    rows, columns = activations.shape[0], adapter_down.shape[1]
    pieces = 4
    return pl.pallas_call(
        low_kernel,
        in_specs=[pl.BlockSpec(memory_space=pltpu.HBM)] * 2,
        out_specs=(whole(), whole()),
        out_shape=(
            jax.ShapeDtypeStruct((rows, columns), jnp.float32),
            jax.ShapeDtypeStruct((rows, columns), jnp.bfloat16),
        ),
        scratch_shapes=[
            pltpu.VMEM(activations.shape, activations.dtype),
            pltpu.VMEM(adapter_down.shape, adapter_down.dtype),
            pltpu.SemaphoreType.DMA((pieces,)),
            pltpu.SemaphoreType.DMA((pieces,)),
        ],
        compiler_params=pltpu.CompilerParams(vmem_limit_bytes=56 * 1024 * 1024),
        cost_estimate=pl.CostEstimate(flops=1 << 29, bytes_accessed=4 << 20, transcendentals=0),
    )(activations, adapter_down)


def add_kernel(low_ref, got_ref, sum_ref, sent_ref):
    total = low_ref[...] + got_ref[...].astype(jnp.float32)
    sum_ref[...] = total
    sent_ref[...] = total.astype(jnp.bfloat16)


def gated(low, more, coef):
    return ((low + more.astype(jnp.float32)) * coef).astype(jnp.bfloat16)


def kv_kernel(group_ref, low_ref, more_ref, coef_ref, upk_ref, upv_ref, kb_ref, vb_ref, cos_ref, sin_ref, mine_ref, other_ref, gq_ref):
    group = group_ref[0]
    coef = coef_ref[...]
    gq_ref[...], gk, gv = [
        gated(low_ref[:, p * SPAN : (p + 1) * SPAN], more_ref[:, p * SPAN : (p + 1) * SPAN], coef) for p in range(3)
    ]
    key_raw = kb_ref[...].astype(jnp.float32) + jnp.dot(gk, upk_ref[...], preferred_element_type=jnp.float32)
    value = vb_ref[...].astype(jnp.float32) + jnp.dot(gv, upv_ref[...], preferred_element_type=jnp.float32)
    cosine, sine = cos_ref[...], sin_ref[...]
    keys = [turn(key_raw[:, h * HD : (h + 1) * HD], cosine, sine) for h in range(2)]
    values = [value[:, h * HD : (h + 1) * HD] for h in range(2)]
    first = group == 0
    mine_ref[:, :HD] = jnp.where(first, keys[0], keys[1]).astype(jnp.bfloat16)
    mine_ref[:, HD:] = jnp.where(first, values[0], values[1]).astype(jnp.bfloat16)
    other_ref[:, :HD] = jnp.where(first, keys[1], keys[0]).astype(jnp.bfloat16)
    other_ref[:, HD:] = jnp.where(first, values[1], values[0]).astype(jnp.bfloat16)


def q_kernel(group_ref, gq_ref, upq_ref, qb_ref, cos_ref, sin_ref, mine_ref, *other_refs):
    own = group_ref[0]
    cosine, sine = cos_ref[...], sin_ref[...]
    gq = gq_ref[...]
    start = (1 - own) * GROUP
    for target in (*other_refs, mine_ref):
        heads = target.shape[1] // HD
        if target is mine_ref:
            start = own * GROUP
        for j in range(heads):
            cols = pl.ds(pl.multiple_of((start + j) * HD, HD), HD)
            raw = qb_ref[:, cols].astype(jnp.float32) + jnp.dot(
                gq, upq_ref[:, cols], preferred_element_type=jnp.float32
            )
            target[:, j * HD : (j + 1) * HD] = turn(raw, cosine, sine).astype(jnp.bfloat16)
        start = start + heads


def join_kernel(*refs):
    *parts, out_ref = refs
    start = 0
    for part in parts:
        out_ref[start : start + part.shape[0]] = part[...]
        start += part.shape[0]


def touch_kernel(seen_ref, in_ref, out_ref):
    out_ref[...] = in_ref[...]


def queries(refs):
    tiles = [ref[:, g * HD : (g + 1) * HD] for ref in refs for g in range(ref.shape[1] // HD)]
    return jnp.concatenate(tiles, axis=0)


def scores_of(keys, query):
    return lax.dot_general(keys, query, (((1,), (1,)), ((), ())), preferred_element_type=jnp.float32)


def weighted(values, weights):
    return lax.dot_general(values, weights, (((0,), (0,)), ((), ())), preferred_element_type=jnp.float32)


def careful(q_sides, kv_refs, states, spare, bases=None):
    gap = lax.broadcasted_iota(jnp.int32, (ROWS, HD), 1) - lax.broadcasted_iota(jnp.int32, (ROWS, HD), 0)
    q_ref, kv_ref = spare
    start = 0
    for ref in kv_refs:
        kv_ref[start : start + ref.shape[0]] = ref[...]
        start += ref.shape[0]
    for q_refs, (top_ref, total_ref, acc_ref) in zip(q_sides, states):
        start = 0
        for ref in q_refs:
            q_ref[:, start : start + ref.shape[1]] = ref[...]
            start += ref.shape[1]

        def body(i, carry, top_ref=top_ref, total_ref=total_ref, acc_ref=acc_ref):
            j, g = i // GROUP, i % GROUP
            rows = pl.ds(pl.multiple_of(j * ROWS, ROWS), ROWS)
            cols = pl.ds(pl.multiple_of(g * HD, HD), HD)
            scores = scores_of(kv_ref[rows, :HD], q_ref[:, cols])
            if bases is not None:
                scores = jnp.where(gap >= bases[j] - bases[SLAB // ROWS], scores, floor_value)
            old = top_ref[:, cols]
            top = jnp.maximum(old, jnp.max(scores, axis=0, keepdims=True) * FACTOR)
            expo = jnp.exp2(scores * FACTOR - top[:1])
            shrink = jnp.exp2(old - top)
            top_ref[:, cols] = top
            total_ref[:, cols] = total_ref[:, cols] * shrink + jnp.sum(expo.reshape(ROWS // 8, 8, HD), axis=0)
            acc_ref[:, cols] = acc_ref[:, cols] * shrink[:1] + weighted(kv_ref[rows, HD:], expo.astype(jnp.bfloat16))
            return carry

        lax.fori_loop(0, SLAB // ROWS * GROUP, body, 0)


def first_kernel(diagonal, base_ref, *refs):
    *q_refs, a_ref, b_ref, top_ref, total_ref, acc_ref, spare_q, spare_kv = refs
    kv = jnp.concatenate([a_ref[...], b_ref[...]], axis=0)
    scores = scores_of(kv[:, :HD], queries(q_refs))
    gap = lax.broadcasted_iota(jnp.int32, (ROWS, HD), 1) - lax.broadcasted_iota(jnp.int32, (ROWS, HD), 0)
    lines = [scores[j * ROWS : (j + 1) * ROWS] for j in range(SLAB // ROWS)]
    seen = jnp.concatenate([gap >= 0] * GROUP, axis=1)
    lines[diagonal] = jnp.where(seen, lines[diagonal], floor_value)
    top = jnp.max(lines[diagonal], axis=0, keepdims=True) * FACTOR
    top = jnp.broadcast_to(top, (8, SIDE))
    parts = []
    for j, line in enumerate(lines):
        hidden = jnp.where(base_ref[j] > base_ref[SLAB // ROWS], -floor_value, 0.0)
        parts.append(jnp.exp2(line.reshape(ROWS // 8, 8, SIDE) * FACTOR - (top + hidden)[None]))
    expo = jnp.concatenate(parts, axis=0)
    total = jnp.sum(expo, axis=0)
    top_ref[...] = top
    total_ref[...] = total
    acc_ref[...] = weighted(kv[:, HD:], expo.astype(jnp.bfloat16).reshape(SLAB, SIDE))

    @pl.when(jnp.logical_not(jnp.max(total) <= ROOM))
    def _():
        total_ref[...] = jnp.zeros_like(total_ref)
        acc_ref[...] = jnp.zeros_like(acc_ref)
        careful([q_refs], (a_ref, b_ref), [(top_ref, total_ref, acc_ref)], (spare_q, spare_kv), base_ref)


def part_of(query, kv, top):
    keys, cols = kv.shape[0], query.shape[0]
    scores = scores_of(kv[:, :HD], query).reshape(keys // 8, 8, cols)
    expo = jnp.exp2(scores * FACTOR - top[None])
    total = jnp.sum(expo, axis=0)
    acc = weighted(kv[:, HD:], expo.astype(jnp.bfloat16).reshape(keys, cols))
    return total, acc, jnp.max(total) <= ROOM


def next_kernel(flag_ref, *refs):
    q_refs, kv_ref, ins, outs, spare, part_ref = refs[:3], refs[3], refs[4:10], refs[10:16], refs[16:18], refs[18]

    @pl.when(flag_ref[0] == 0)
    def _():
        for ref, given in zip(outs, ins):
            ref[...] = given[...]

    @pl.when(flag_ref[0] != 0)
    def _():
        top = jnp.concatenate([ins[0][...], ins[3][...]], axis=1)
        total, part_ref[...], room = part_of(queries(q_refs), kv_ref[...], top)

        @pl.when(room)
        def _():
            for side in range(2):
                cols = slice(side * SIDE, (side + 1) * SIDE)
                outs[3 * side][...] = ins[3 * side][...]
                outs[3 * side + 1][...] = ins[3 * side + 1][...] + total[:, cols]
                outs[3 * side + 2][...] = ins[3 * side + 2][...] + part_ref[:, cols]

        @pl.when(jnp.logical_not(room))
        def _():
            for ref, given in zip(outs, ins):
                ref[...] = given[...]
            careful([q_refs[:1], q_refs[1:]], (kv_ref,), [outs[:3], outs[3:]], spare)


def loop_kernel(flag_ref, *refs):
    q_refs, kv_ref, ins, outs, spare = refs[:3], refs[3], refs[4:10], refs[10:16], refs[16:18]
    sides_q, tops, totals, accs = refs[18:]

    @pl.when(flag_ref[0] == 0)
    def _():
        for ref, given in zip(outs, ins):
            ref[...] = given[...]

    @pl.when(flag_ref[0] != 0)
    def _():
        sides_q[0] = q_refs[0][...]
        sides_q[1, :, : SIDE // 2] = q_refs[1][...]
        sides_q[1, :, SIDE // 2 :] = q_refs[2][...]
        for side in range(2):
            tops[side] = ins[3 * side][...]

        def body(side, carry):
            totals[side], accs[side], unused = part_of(queries([sides_q.at[side]]), kv_ref[...], tops[side])
            return carry

        lax.fori_loop(0, 2, body, 0)
        room = jnp.max(totals[...]) <= ROOM

        @pl.when(room)
        def _():
            for side in range(2):
                outs[3 * side][...] = ins[3 * side][...]
                outs[3 * side + 1][...] = ins[3 * side + 1][...] + totals[side]
                outs[3 * side + 2][...] = ins[3 * side + 2][...] + accs[side]

        @pl.when(jnp.logical_not(room))
        def _():
            for ref, given in zip(outs, ins):
                ref[...] = given[...]
            careful([q_refs[:1], q_refs[1:]], (kv_ref,), [outs[:3], outs[3:]], spare)


def last_kernel(flag_ref, *refs):
    *q_refs, a_ref, b_ref, top_ref, total_ref, acc_ref, out_ref, spare_q, spare_kv, last_top, last_total, last_acc = refs
    last_total[...] = total_ref[...]
    last_acc[...] = acc_ref[...]

    @pl.when(flag_ref[0] != 0)
    def _():
        kv = jnp.concatenate([a_ref[...], b_ref[...]], axis=0)
        total, acc, room = part_of(queries(q_refs), kv, top_ref[...])
        last_total[...] = total_ref[...] + total
        last_acc[...] = acc_ref[...] + acc

        @pl.when(jnp.logical_not(room))
        def _():
            last_top[...] = top_ref[...]
            last_total[...] = total_ref[...]
            last_acc[...] = acc_ref[...]
            careful([q_refs], (a_ref, b_ref), [(last_top, last_total, last_acc)], (spare_q, spare_kv))

    scale = 1.0 / jnp.sum(last_total[...], axis=0, keepdims=True)
    for g in range(GROUP):
        cols = slice(g * HD, (g + 1) * HD)
        out_ref[:, cols] = (last_acc[:, cols] * scale[:, cols]).T.astype(jnp.bfloat16)


def whole():
    return pl.BlockSpec(memory_space=pltpu.VMEM)


def call(kernel, n_in, outs, n_scalar=1, aliases=None, scratch=()):
    return pl.pallas_call(
        kernel,
        out_shape=outs,
        in_specs=[pl.BlockSpec(memory_space=pltpu.SMEM)] * n_scalar + [whole()] * n_in,
        out_specs=tuple(whole() for _ in outs),
        input_output_aliases=aliases or {},
        scratch_shapes=list(scratch),
        compiler_params=pltpu.CompilerParams(vmem_limit_bytes=VMEM_LIMIT),
        cost_estimate=pl.CostEstimate(flops=1 << 34, bytes_accessed=1 << 26, transcendentals=0),
    )


def after(array, *others):
    return lax.optimization_barrier((array,) + others)


def on_device(activations, adapter_down, adapter_ids, adapter_weight, query_base, key_base, value_base, up_query, up_key, up_value):
    ctx = lax.axis_index("ctx").astype(jnp.int32)
    z, x, core = ctx // (2 * XS), (ctx // 2) % XS, ctx % 2
    group = ((x + 1) // 2) % 2
    groups = group.reshape(1)
    f32, b16 = jnp.float32, jnp.bfloat16
    shape = jax.ShapeDtypeStruct

    low, sent = low_product(activations, adapter_down)

    def pair_up(array, step):
        return send(array, lambda z, x, c, y: (z, x, c, y ^ (1 if c == step else 3)))

    one = pair_up(sent, 0)

    labels = jnp.arange(SPAN, dtype=jnp.int32) // RANK
    coef = jnp.zeros((ROWS, SPAN), f32)
    for j in range(adapter_ids.shape[1]):
        coef = coef + jnp.where(adapter_ids[:, j : j + 1] == labels[None, :], adapter_weight[:, j : j + 1], 0.0)
    positions = (ctx * ROWS + jnp.arange(ROWS, dtype=jnp.int32)).astype(f32)
    inverse = jnp.exp(jnp.arange(HD // 2, dtype=f32) * (-2.0 * math.log(rope_base) / HD))
    angles = positions[:, None] * jnp.concatenate([inverse, inverse])[None, :]
    cosine = jnp.cos(angles)
    sign = jnp.where(jnp.arange(HD) < HD // 2, -1.0, 1.0).astype(f32)
    sine = jnp.sin(angles) * sign[None, :]
    low = call(join_kernel, 1, (shape(low.shape, f32),), 0)(low)[0]
    one, low, coef, cosine, sine = after(one, low, coef, cosine, sine)
    low, sent = call(add_kernel, 2, (shape(low.shape, f32), shape(low.shape, b16)), 0)(low, one)
    two = pair_up(sent, 1)

    kv_shape = shape((ROWS, 2 * HD), b16)
    kv, kv_other, gated_query = call(kv_kernel, 9, (kv_shape, kv_shape, shape((ROWS, SPAN), b16)))(
        groups, low, two, coef, up_key, up_value, key_base, value_base, cosine, sine
    )

    def neighbour(array):
        return send(array, lambda z, x, c, y: (z, x ^ 1, c, y))

    blocks_x = [
        neighbour(kv_other),
        send(kv, lambda z, x, c, y: (z, x ^ 3, c, y)),
        send(kv_other, lambda z, x, c, y: (z, x ^ 2, c, y)),
    ]
    side_shape = shape((ROWS, GROUP * HD), b16)
    piece_shape = shape((ROWS, GROUP * HD // 2), b16)
    q_own, *q_other = call(q_kernel, 5, (side_shape, piece_shape, piece_shape))(
        groups, gated_query, up_query, query_base, cosine, sine
    )
    *blocks_x, q_own, q_first, q_second = after(*blocks_x, q_own, *q_other)

    def join(*parts):
        rows = sum(part.shape[0] for part in parts)
        return call(join_kernel, len(parts), (shape((rows, 2 * HD), b16),), 0)(*parts)[0]

    moving_a = join(kv, *blocks_x)
    q_rest = [neighbour(q_first), neighbour(q_second)]

    def ring(array):
        return send(array, lambda z, x, c, y: (z + (1 if c == 0 else -1), x, c, y))

    arriving_a = ring(moving_a)
    moving_b = swap_cores(moving_a)
    moving_b, q_rest[0] = after(moving_b, q_rest[0])
    arriving_b = ring(moving_b)

    blocks = (jnp.stack([x, x ^ 1, x ^ 3, x ^ 2]) - x) * BLOCK
    keys_at = jnp.concatenate([blocks + core * ROWS, blocks + (1 - core) * ROWS])

    def bases(start):
        return jnp.concatenate([keys_at, start.reshape(1)]).astype(jnp.int32)

    spare = [pltpu.VMEM((ROWS, SIDE), b16), pltpu.VMEM((SLAB, 2 * HD), b16)]
    state_shape = (shape((8, SIDE), f32), shape((8, SIDE), f32), shape((HD, SIDE), f32))
    state = [
        *call(functools.partial(first_kernel, 0), 3, state_shape, scratch=spare)(bases(core * ROWS), q_own, moving_a, moving_b),
    ]
    state += call(functools.partial(first_kernel, 1), 4, state_shape, scratch=spare)(
        bases(((x ^ 1) - x) * BLOCK + core * ROWS), *q_rest, moving_a, moving_b
    )

    def attend(kernel, scratch, flag, kv, state):
        aliases = {5 + k: k for k in range(6)}
        return call(kernel, 10, state_shape * 2, 1, aliases, spare + scratch)(
            flag.astype(jnp.int32).reshape(1), q_own, *q_rest, kv, *state
        )

    near = functools.partial(attend, next_kernel, [pltpu.VMEM((HD, 2 * SIDE), f32)])
    sides = [((2, ROWS, SIDE), b16), ((2, 8, SIDE), f32), ((2, 8, SIDE), f32), ((2, HD, SIDE), f32)]
    away = functools.partial(attend, loop_kernel, [pltpu.VMEM(*side) for side in sides])

    def take(arriving, state, on):
        arrived, *state = after(arriving, *state)
        if not on:
            return arrived, None, state
        arriving = ring(arrived)
        top = call(touch_kernel, 2, state_shape[:1], 0, {1: 0})(arrived, state[0])[0]
        return arrived, arriving, [top, *state[1:]]

    next_a, arriving_a, state = take(arriving_a, state, True)
    for step in range(1, 4):
        below, wrapped = z >= step, z + step >= ZS
        moving_b, arriving_b, state = take(arriving_b, state, True)
        moving = join(next_a, moving_b)
        swapped = swap_cores(moving)
        state = near(jnp.where(core == 0, below, wrapped), moving, state)
        next_a, arriving_a, state = take(arriving_a, state, step < 3)
        state = away(jnp.where(core == 0, wrapped, below), swapped, state)
    moving_a = next_a
    moving_b, *state = after(arriving_b, *state)
    flag = (z >= ZS // 2).astype(jnp.int32).reshape(1)

    def finish(query, state):
        scratch = spare + [pltpu.VMEM((8, SIDE), f32)] * 2 + [pltpu.VMEM((HD, SIDE), f32)]
        return call(last_kernel, len(query) + 5, (side_shape,), scratch=scratch)(
            flag, *query, moving_a, moving_b, *state
        )[0]

    back = neighbour(finish(q_rest, state[3:]))
    own = finish([q_own], state[:3])
    return jnp.concatenate([jnp.where(group == 0, own, back), jnp.where(group == 0, back, own)], axis=1)


def solution(mesh):
    in_specs = (
        P("ctx", "head"),
        P("head", None),
        P("ctx", None),
        P("ctx", None),
        P("ctx", "head"),
        P("ctx", "head"),
        P("ctx", "head"),
        P(None, "head"),
        P(None, "head"),
        P(None, "head"),
    )
    return jax.shard_map(on_device, mesh=mesh, in_specs=in_specs, out_specs=P("ctx", "head"), check_vma=False)
```

```python
import functools
import math

import jax
import jax.numpy as jnp
from jax import lax
from jax.experimental import pallas as pl
from jax.experimental.pallas import tpu as pltpu
from jax.sharding import PartitionSpec as P

HD = 128
ADAPTERS = 8
RANK = 32
SPAN = ADAPTERS * RANK
ROWS = 128
GROUP = 8
ZS, XS, YS = 8, 4, 4
BLOCK = 2 * ROWS
SLAB = XS * BLOCK
SIDE = GROUP * ROWS

rope_base = 500000.0
floor_value = -1e30
FACTOR = math.log2(math.e) / math.sqrt(HD)
ROOM = 2.0**60
VMEM_LIMIT = 40 * 1024 * 1024


def device(z, x, core, y):
    return (((z % ZS) * XS + x % XS) * 2 + core) * YS + y


def send(array, move):
    pairs = []
    for z in range(ZS):
        for x in range(XS):
            for core in range(2):
                for y in range(YS):
                    target = move(z, x, core, y)
                    if target is not None:
                        pairs.append((device(z, x, core, y), device(*target)))
    return lax.ppermute(array, ("ctx", "head"), pairs)


def swap_cores(array):
    return send(array, lambda z, x, core, y: (z, x, 1 - core, y))


def turn(raw, cosine, sine):
    return raw * cosine + pltpu.roll(raw, HD // 2, 1) * sine


def low_kernel(act_hbm, down_hbm, low_ref, sent_ref, act_ref, down_ref, act_sem, down_sem):
    pieces = act_sem.shape[0]
    depth = act_ref.shape[1] // pieces
    copies = []
    for k in range(pieces):
        span = slice(k * depth, (k + 1) * depth)
        copies.append(
            (
                pltpu.make_async_copy(act_hbm.at[:, span], act_ref.at[:, span], act_sem.at[k]),
                pltpu.make_async_copy(down_hbm.at[span], down_ref.at[span], down_sem.at[k]),
            )
        )
        for copy in copies[-1]:
            copy.start()
    total = None
    for k in range(pieces):
        span = slice(k * depth, (k + 1) * depth)
        for copy in copies[k]:
            copy.wait()
        part = jnp.dot(act_ref[:, span], down_ref[span], preferred_element_type=jnp.float32)
        total = part if total is None else total + part
    low_ref[...] = total
    sent_ref[...] = total.astype(jnp.bfloat16)


def low_product(activations, adapter_down):
    rows, columns = activations.shape[0], adapter_down.shape[1]
    pieces = 4
    return pl.pallas_call(
        low_kernel,
        in_specs=[pl.BlockSpec(memory_space=pltpu.HBM)] * 2,
        out_specs=(whole(), whole()),
        out_shape=(
            jax.ShapeDtypeStruct((rows, columns), jnp.float32),
            jax.ShapeDtypeStruct((rows, columns), jnp.bfloat16),
        ),
        scratch_shapes=[
            pltpu.VMEM(activations.shape, activations.dtype),
            pltpu.VMEM(adapter_down.shape, adapter_down.dtype),
            pltpu.SemaphoreType.DMA((pieces,)),
            pltpu.SemaphoreType.DMA((pieces,)),
        ],
        compiler_params=pltpu.CompilerParams(vmem_limit_bytes=56 * 1024 * 1024),
        cost_estimate=pl.CostEstimate(flops=1 << 29, bytes_accessed=4 << 20, transcendentals=0),
    )(activations, adapter_down)


def add_kernel(low_ref, got_ref, sum_ref, sent_ref):
    total = low_ref[...] + got_ref[...].astype(jnp.float32)
    sum_ref[...] = total
    sent_ref[...] = total.astype(jnp.bfloat16)


def gated(low, more, coef):
    return ((low + more.astype(jnp.float32)) * coef).astype(jnp.bfloat16)


def kv_kernel(group_ref, low_ref, more_ref, coef_ref, upk_ref, upv_ref, kb_ref, vb_ref, cos_ref, sin_ref, mine_ref, other_ref, gq_ref):
    group = group_ref[0]
    coef = coef_ref[...]
    gq_ref[...], gk, gv = [
        gated(low_ref[:, p * SPAN : (p + 1) * SPAN], more_ref[:, p * SPAN : (p + 1) * SPAN], coef) for p in range(3)
    ]
    key_raw = kb_ref[...].astype(jnp.float32) + jnp.dot(gk, upk_ref[...], preferred_element_type=jnp.float32)
    value = vb_ref[...].astype(jnp.float32) + jnp.dot(gv, upv_ref[...], preferred_element_type=jnp.float32)
    cosine, sine = cos_ref[...], sin_ref[...]
    keys = [turn(key_raw[:, h * HD : (h + 1) * HD], cosine, sine) for h in range(2)]
    values = [value[:, h * HD : (h + 1) * HD] for h in range(2)]
    first = group == 0
    mine_ref[:, :HD] = jnp.where(first, keys[0], keys[1]).astype(jnp.bfloat16)
    mine_ref[:, HD:] = jnp.where(first, values[0], values[1]).astype(jnp.bfloat16)
    other_ref[:, :HD] = jnp.where(first, keys[1], keys[0]).astype(jnp.bfloat16)
    other_ref[:, HD:] = jnp.where(first, values[1], values[0]).astype(jnp.bfloat16)


def q_kernel(group_ref, gq_ref, upq_ref, qb_ref, cos_ref, sin_ref, mine_ref, *other_refs):
    own = group_ref[0]
    cosine, sine = cos_ref[...], sin_ref[...]
    gq = gq_ref[...]
    start = (1 - own) * GROUP
    for target in (*other_refs, mine_ref):
        heads = target.shape[1] // HD
        if target is mine_ref:
            start = own * GROUP
        for j in range(heads):
            cols = pl.ds(pl.multiple_of((start + j) * HD, HD), HD)
            raw = qb_ref[:, cols].astype(jnp.float32) + jnp.dot(
                gq, upq_ref[:, cols], preferred_element_type=jnp.float32
            )
            target[:, j * HD : (j + 1) * HD] = turn(raw, cosine, sine).astype(jnp.bfloat16)
        start = start + heads


def join_kernel(*refs):
    *parts, out_ref = refs
    start = 0
    for part in parts:
        out_ref[start : start + part.shape[0]] = part[...]
        start += part.shape[0]


def touch_kernel(seen_ref, in_ref, out_ref):
    out_ref[...] = in_ref[...]


def queries(refs):
    tiles = [ref[:, g * HD : (g + 1) * HD] for ref in refs for g in range(ref.shape[1] // HD)]
    return jnp.concatenate(tiles, axis=0)


def scores_of(keys, query):
    return lax.dot_general(keys, query, (((1,), (1,)), ((), ())), preferred_element_type=jnp.float32)


def weighted(values, weights):
    return lax.dot_general(values, weights, (((0,), (0,)), ((), ())), preferred_element_type=jnp.float32)


def careful(q_sides, kv_refs, states, spare, bases=None):
    gap = lax.broadcasted_iota(jnp.int32, (ROWS, HD), 1) - lax.broadcasted_iota(jnp.int32, (ROWS, HD), 0)
    q_ref, kv_ref = spare
    start = 0
    for ref in kv_refs:
        kv_ref[start : start + ref.shape[0]] = ref[...]
        start += ref.shape[0]
    for q_refs, (top_ref, total_ref, acc_ref) in zip(q_sides, states):
        start = 0
        for ref in q_refs:
            q_ref[:, start : start + ref.shape[1]] = ref[...]
            start += ref.shape[1]

        def body(i, carry, top_ref=top_ref, total_ref=total_ref, acc_ref=acc_ref):
            j, g = i // GROUP, i % GROUP
            rows = pl.ds(pl.multiple_of(j * ROWS, ROWS), ROWS)
            cols = pl.ds(pl.multiple_of(g * HD, HD), HD)
            scores = scores_of(kv_ref[rows, :HD], q_ref[:, cols])
            if bases is not None:
                scores = jnp.where(gap >= bases[j] - bases[SLAB // ROWS], scores, floor_value)
            old = top_ref[:, cols]
            top = jnp.maximum(old, jnp.max(scores, axis=0, keepdims=True) * FACTOR)
            expo = jnp.exp2(scores * FACTOR - top[:1])
            shrink = jnp.exp2(old - top)
            top_ref[:, cols] = top
            total_ref[:, cols] = total_ref[:, cols] * shrink + jnp.sum(expo.reshape(ROWS // 8, 8, HD), axis=0)
            acc_ref[:, cols] = acc_ref[:, cols] * shrink[:1] + weighted(kv_ref[rows, HD:], expo.astype(jnp.bfloat16))
            return carry

        lax.fori_loop(0, SLAB // ROWS * GROUP, body, 0)


def first_kernel(diagonal, base_ref, *refs):
    *q_refs, a_ref, b_ref, top_ref, total_ref, acc_ref, spare_q, spare_kv = refs
    kv = jnp.concatenate([a_ref[...], b_ref[...]], axis=0)
    scores = scores_of(kv[:, :HD], queries(q_refs))
    gap = lax.broadcasted_iota(jnp.int32, (ROWS, HD), 1) - lax.broadcasted_iota(jnp.int32, (ROWS, HD), 0)
    lines = [scores[j * ROWS : (j + 1) * ROWS] for j in range(SLAB // ROWS)]
    seen = jnp.concatenate([gap >= 0] * GROUP, axis=1)
    lines[diagonal] = jnp.where(seen, lines[diagonal], floor_value)
    top = jnp.max(lines[diagonal], axis=0, keepdims=True) * FACTOR
    top = jnp.broadcast_to(top, (8, SIDE))
    parts = []
    for j, line in enumerate(lines):
        hidden = jnp.where(base_ref[j] > base_ref[SLAB // ROWS], -floor_value, 0.0)
        parts.append(jnp.exp2(line.reshape(ROWS // 8, 8, SIDE) * FACTOR - (top + hidden)[None]))
    expo = jnp.concatenate(parts, axis=0)
    total = jnp.sum(expo, axis=0)
    top_ref[...] = top
    total_ref[...] = total
    acc_ref[...] = weighted(kv[:, HD:], expo.astype(jnp.bfloat16).reshape(SLAB, SIDE))

    @pl.when(jnp.logical_not(jnp.max(total) <= ROOM))
    def _():
        total_ref[...] = jnp.zeros_like(total_ref)
        acc_ref[...] = jnp.zeros_like(acc_ref)
        careful([q_refs], (a_ref, b_ref), [(top_ref, total_ref, acc_ref)], (spare_q, spare_kv), base_ref)


def part_of(query, kv, top):
    keys, cols = kv.shape[0], query.shape[0]
    scores = scores_of(kv[:, :HD], query).reshape(keys // 8, 8, cols)
    expo = jnp.exp2(scores * FACTOR - top[None])
    total = jnp.sum(expo, axis=0)
    acc = weighted(kv[:, HD:], expo.astype(jnp.bfloat16).reshape(keys, cols))
    return total, acc, jnp.max(total) <= ROOM


def next_kernel(flag_ref, *refs):
    q_refs, kv_ref, ins, outs, spare, part_ref = refs[:2], refs[2], refs[3:9], refs[9:15], refs[15:17], refs[17]

    @pl.when(flag_ref[0] == 0)
    def _():
        for ref, given in zip(outs, ins):
            ref[...] = given[...]

    @pl.when(flag_ref[0] != 0)
    def _():
        top = jnp.concatenate([ins[0][...], ins[3][...]], axis=1)
        total, part_ref[...], room = part_of(queries(q_refs), kv_ref[...], top)

        @pl.when(room)
        def _():
            for side in range(2):
                cols = slice(side * SIDE, (side + 1) * SIDE)
                outs[3 * side][...] = ins[3 * side][...]
                outs[3 * side + 1][...] = ins[3 * side + 1][...] + total[:, cols]
                outs[3 * side + 2][...] = ins[3 * side + 2][...] + part_ref[:, cols]

        @pl.when(jnp.logical_not(room))
        def _():
            for ref, given in zip(outs, ins):
                ref[...] = given[...]
            careful([q_refs[:1], q_refs[1:]], (kv_ref,), [outs[:3], outs[3:]], spare)


def last_kernel(flag_ref, *refs):
    *q_refs, a_ref, b_ref, top_ref, total_ref, acc_ref, out_ref, spare_q, spare_kv, last_top, last_total, last_acc = refs
    last_total[...] = total_ref[...]
    last_acc[...] = acc_ref[...]

    @pl.when(flag_ref[0] != 0)
    def _():
        kv = jnp.concatenate([a_ref[...], b_ref[...]], axis=0)
        total, acc, room = part_of(queries(q_refs), kv, top_ref[...])
        last_total[...] = total_ref[...] + total
        last_acc[...] = acc_ref[...] + acc

        @pl.when(jnp.logical_not(room))
        def _():
            last_top[...] = top_ref[...]
            last_total[...] = total_ref[...]
            last_acc[...] = acc_ref[...]
            careful([q_refs], (a_ref, b_ref), [(last_top, last_total, last_acc)], (spare_q, spare_kv))

    scale = 1.0 / jnp.sum(last_total[...], axis=0, keepdims=True)
    for g in range(GROUP):
        cols = slice(g * HD, (g + 1) * HD)
        out_ref[:, cols] = (last_acc[:, cols] * scale[:, cols]).T.astype(jnp.bfloat16)


def whole():
    return pl.BlockSpec(memory_space=pltpu.VMEM)


def call(kernel, n_in, outs, n_scalar=1, aliases=None, scratch=(), flops=1 << 16):
    return pl.pallas_call(
        kernel,
        out_shape=outs,
        in_specs=[pl.BlockSpec(memory_space=pltpu.SMEM)] * n_scalar + [whole()] * n_in,
        out_specs=tuple(whole() for _ in outs),
        input_output_aliases=aliases or {},
        scratch_shapes=list(scratch),
        compiler_params=pltpu.CompilerParams(vmem_limit_bytes=VMEM_LIMIT),
        cost_estimate=pl.CostEstimate(flops=flops, bytes_accessed=flops >> 8, transcendentals=0),
    )


def after(array, *others):
    return lax.optimization_barrier((array,) + others)


def touch(seen, array, flops=1 << 34):
    out = jax.ShapeDtypeStruct(array.shape, array.dtype)
    return call(touch_kernel, 2, (out,), 0, {1: 0}, flops=flops)(seen, array)[0]


def on_device(activations, adapter_down, adapter_ids, adapter_weight, query_base, key_base, value_base, up_query, up_key, up_value):
    ctx = lax.axis_index("ctx").astype(jnp.int32)
    z, x, core = ctx // (2 * XS), (ctx // 2) % XS, ctx % 2
    group = ((x + 1) // 2) % 2
    groups = group.reshape(1)
    f32, b16 = jnp.float32, jnp.bfloat16
    shape = jax.ShapeDtypeStruct

    low, sent = low_product(activations, adapter_down)

    def pair_up(array, step):
        return send(array, lambda z, x, c, y: (z, x, c, y ^ (1 if c == step else 3)))

    one = pair_up(sent, 0)

    labels = jnp.arange(SPAN, dtype=jnp.int32) // RANK
    coef = jnp.zeros((ROWS, SPAN), f32)
    for j in range(adapter_ids.shape[1]):
        coef = coef + jnp.where(adapter_ids[:, j : j + 1] == labels[None, :], adapter_weight[:, j : j + 1], 0.0)
    positions = (ctx * ROWS + jnp.arange(ROWS, dtype=jnp.int32)).astype(f32)
    inverse = jnp.exp(jnp.arange(HD // 2, dtype=f32) * (-2.0 * math.log(rope_base) / HD))
    angles = positions[:, None] * jnp.concatenate([inverse, inverse])[None, :]
    cosine = jnp.cos(angles)
    sign = jnp.where(jnp.arange(HD) < HD // 2, -1.0, 1.0).astype(f32)
    sine = jnp.sin(angles) * sign[None, :]
    low = call(join_kernel, 1, (shape(low.shape, f32),), 0)(low)[0]
    one, low, coef, cosine, sine = after(one, low, coef, cosine, sine)
    low, sent = call(add_kernel, 2, (shape(low.shape, f32), shape(low.shape, b16)), 0)(low, one)
    two = pair_up(sent, 1)

    kv_shape = shape((ROWS, 2 * HD), b16)
    kv, kv_other, gated_query = call(kv_kernel, 9, (kv_shape, kv_shape, shape((ROWS, SPAN), b16)))(
        groups, low, two, coef, up_key, up_value, key_base, value_base, cosine, sine
    )

    def neighbour(array):
        return send(array, lambda z, x, c, y: (z, x ^ 1, c, y))

    blocks_x = [
        neighbour(kv_other),
        send(kv, lambda z, x, c, y: (z, x ^ 3, c, y)),
        send(kv_other, lambda z, x, c, y: (z, x ^ 2, c, y)),
    ]
    side_shape = shape((ROWS, GROUP * HD), b16)
    q_own, q_other = call(q_kernel, 5, (side_shape, side_shape))(
        groups, gated_query, up_query, query_base, cosine, sine
    )
    q_rest = neighbour(q_other)
    q_own = touch(q_other, q_own, 1 << 36)
    *blocks_x, q_own = after(*blocks_x, q_own)

    def join(*parts):
        rows = sum(part.shape[0] for part in parts)
        return call(join_kernel, len(parts), (shape((rows, 2 * HD), b16),), 0)(*parts)[0]

    moving_a = join(kv, *blocks_x)

    def onward(step):
        def move(z, x, core, y):
            if core == 0:
                return (z + 1, x, core, y) if step - 1 <= z < ZS - 1 else None
            return (z - 1, x, core, y) if (z + step - 1) % ZS < ZS // 2 else None

        return move

    def ring(array, step):
        return send(array, onward(step))

    arriving_a = ring(moving_a, 1)
    moving_b = swap_cores(moving_a)
    arriving_b = ring(moving_b, 1)
    q_own = touch(moving_b, q_own, 1 << 30)

    blocks = (jnp.stack([x, x ^ 1, x ^ 3, x ^ 2]) - x) * BLOCK
    keys_at = jnp.concatenate([blocks + core * ROWS, blocks + (1 - core) * ROWS])

    def bases(start):
        return jnp.concatenate([keys_at, start.reshape(1)]).astype(jnp.int32)

    spare = [pltpu.VMEM((ROWS, SIDE), b16), pltpu.VMEM((SLAB, 2 * HD), b16)]
    state_shape = (shape((8, SIDE), f32), shape((8, SIDE), f32), shape((HD, SIDE), f32))
    state = [
        *call(functools.partial(first_kernel, 0), 3, state_shape, scratch=spare)(bases(core * ROWS), q_own, moving_a, moving_b),
    ]
    q_rest, *state = after(q_rest, *state)
    state += call(functools.partial(first_kernel, 1), 3, state_shape, scratch=spare)(
        bases(((x ^ 1) - x) * BLOCK + core * ROWS), q_rest, moving_a, moving_b
    )

    def attend(flag, kv, state):
        aliases = {4 + k: k for k in range(6)}
        scratch = [*spare, pltpu.VMEM((HD, 2 * SIDE), f32)]
        return call(next_kernel, 9, state_shape * 2, 1, aliases, scratch)(
            flag.astype(jnp.int32).reshape(1), q_own, q_rest, kv, *state
        )

    def take(arriving, state, step, flops=1 << 34):
        arrived, *state = after(arriving, *state)
        if step > 4:
            return arrived, None, state
        arriving = ring(arrived, step)
        return arrived, arriving, [touch(arrived, state[0], flops), *state[1:]]

    moving_a, arriving_a, state = take(arriving_a, state, 2, 1 << 31)
    for step in range(1, 4):
        below, wrapped = z >= step, z + step >= ZS
        moving_b, arriving_b, state = take(arriving_b, state, step + 1)
        moving = join(moving_a, moving_b)
        swapped = swap_cores(moving)
        state = attend(jnp.where(core == 0, below, wrapped), moving, state)
        moving_a, arriving_a, state = take(arriving_a, state, step + 2)
        state = attend(jnp.where(core == 0, wrapped, below), swapped, state)
    moving_b, *state = after(arriving_b, *state)
    flag = (z >= ZS // 2).astype(jnp.int32).reshape(1)

    def finish(query, state):
        scratch = spare + [pltpu.VMEM((8, SIDE), f32)] * 2 + [pltpu.VMEM((HD, SIDE), f32)]
        return call(last_kernel, 6, (side_shape,), scratch=scratch)(
            flag, query, moving_a, moving_b, *state
        )[0]

    back = neighbour(finish(q_rest, state[3:]))
    own = finish(q_own, state[:3])
    return jnp.concatenate([jnp.where(group == 0, own, back), jnp.where(group == 0, back, own)], axis=1)


def solution(mesh):
    in_specs = (
        P("ctx", "head"),
        P("head", None),
        P("ctx", None),
        P("ctx", None),
        P("ctx", "head"),
        P("ctx", "head"),
        P("ctx", "head"),
        P(None, "head"),
        P(None, "head"),
        P(None, "head"),
    )
    return jax.shard_map(on_device, mesh=mesh, in_specs=in_specs, out_specs=P("ctx", "head"), check_vma=False)
```

```python
import functools
import math

import jax
import jax.numpy as jnp
from jax import lax
from jax.experimental import pallas as pl
from jax.experimental.pallas import tpu as pltpu
from jax.sharding import PartitionSpec as P

HD = 128
ADAPTERS = 8
RANK = 32
SPAN = ADAPTERS * RANK
ROWS = 128
GROUP = 8
ZS, XS, YS = 8, 4, 4
BLOCK = 2 * ROWS
SLAB = XS * BLOCK
SIDE = GROUP * ROWS

rope_base = 500000.0
floor_value = -1e30
FACTOR = math.log2(math.e) / math.sqrt(HD)
ROOM = 2.0**60
VMEM_LIMIT = 40 * 1024 * 1024


def device(z, x, core, y):
    return (((z % ZS) * XS + x % XS) * 2 + core) * YS + y


def send(array, move):
    pairs = []
    for z in range(ZS):
        for x in range(XS):
            for core in range(2):
                for y in range(YS):
                    pairs.append((device(z, x, core, y), device(*move(z, x, core, y))))
    return lax.ppermute(array, ("ctx", "head"), pairs)


def swap_cores(array):
    return send(array, lambda z, x, core, y: (z, x, 1 - core, y))


def turn(raw, cosine, sine):
    return raw * cosine + pltpu.roll(raw, HD // 2, 1) * sine


def low_kernel(act_hbm, down_hbm, low_ref, sent_ref, act_ref, down_ref, act_sem, down_sem):
    pieces = act_sem.shape[0]
    depth = act_ref.shape[1] // pieces
    copies = []
    for k in range(pieces):
        span = slice(k * depth, (k + 1) * depth)
        copies.append(
            (
                pltpu.make_async_copy(act_hbm.at[:, span], act_ref.at[:, span], act_sem.at[k]),
                pltpu.make_async_copy(down_hbm.at[span], down_ref.at[span], down_sem.at[k]),
            )
        )
        for copy in copies[-1]:
            copy.start()
    total = None
    for k in range(pieces):
        span = slice(k * depth, (k + 1) * depth)
        for copy in copies[k]:
            copy.wait()
        part = jnp.dot(act_ref[:, span], down_ref[span], preferred_element_type=jnp.float32)
        total = part if total is None else total + part
    low_ref[...] = total
    sent_ref[...] = total.astype(jnp.bfloat16)


def low_product(activations, adapter_down):
    rows, columns = activations.shape[0], adapter_down.shape[1]
    pieces = 4
    return pl.pallas_call(
        low_kernel,
        in_specs=[pl.BlockSpec(memory_space=pltpu.HBM)] * 2,
        out_specs=(whole(), whole()),
        out_shape=(
            jax.ShapeDtypeStruct((rows, columns), jnp.float32),
            jax.ShapeDtypeStruct((rows, columns), jnp.bfloat16),
        ),
        scratch_shapes=[
            pltpu.VMEM(activations.shape, activations.dtype),
            pltpu.VMEM(adapter_down.shape, adapter_down.dtype),
            pltpu.SemaphoreType.DMA((pieces,)),
            pltpu.SemaphoreType.DMA((pieces,)),
        ],
        compiler_params=pltpu.CompilerParams(vmem_limit_bytes=56 * 1024 * 1024),
        cost_estimate=pl.CostEstimate(flops=1 << 29, bytes_accessed=4 << 20, transcendentals=0),
    )(activations, adapter_down)


def add_kernel(low_ref, got_ref, sum_ref, sent_ref):
    total = low_ref[...] + got_ref[...].astype(jnp.float32)
    sum_ref[...] = total
    sent_ref[...] = total.astype(jnp.bfloat16)


def gated(low, more, coef):
    return ((low + more.astype(jnp.float32)) * coef).astype(jnp.bfloat16)


def kv_kernel(group_ref, low_ref, more_ref, coef_ref, upk_ref, upv_ref, kb_ref, vb_ref, cos_ref, sin_ref, mine_ref, other_ref, gq_ref):
    group = group_ref[0]
    coef = coef_ref[...]
    gq_ref[...], gk, gv = [
        gated(low_ref[:, p * SPAN : (p + 1) * SPAN], more_ref[:, p * SPAN : (p + 1) * SPAN], coef) for p in range(3)
    ]
    key_raw = kb_ref[...].astype(jnp.float32) + jnp.dot(gk, upk_ref[...], preferred_element_type=jnp.float32)
    value = vb_ref[...].astype(jnp.float32) + jnp.dot(gv, upv_ref[...], preferred_element_type=jnp.float32)
    cosine, sine = cos_ref[...], sin_ref[...]
    keys = [turn(key_raw[:, h * HD : (h + 1) * HD], cosine, sine) for h in range(2)]
    values = [value[:, h * HD : (h + 1) * HD] for h in range(2)]
    first = group == 0
    mine_ref[:, :HD] = jnp.where(first, keys[0], keys[1]).astype(jnp.bfloat16)
    mine_ref[:, HD:] = jnp.where(first, values[0], values[1]).astype(jnp.bfloat16)
    other_ref[:, :HD] = jnp.where(first, keys[1], keys[0]).astype(jnp.bfloat16)
    other_ref[:, HD:] = jnp.where(first, values[1], values[0]).astype(jnp.bfloat16)


def q_kernel(group_ref, gq_ref, upq_ref, qb_ref, cos_ref, sin_ref, mine_ref, *other_refs):
    own = group_ref[0]
    cosine, sine = cos_ref[...], sin_ref[...]
    gq = gq_ref[...]
    start = (1 - own) * GROUP
    for target in (*other_refs, mine_ref):
        heads = target.shape[1] // HD
        if target is mine_ref:
            start = own * GROUP
        for j in range(heads):
            cols = pl.ds(pl.multiple_of((start + j) * HD, HD), HD)
            raw = qb_ref[:, cols].astype(jnp.float32) + jnp.dot(
                gq, upq_ref[:, cols], preferred_element_type=jnp.float32
            )
            target[:, j * HD : (j + 1) * HD] = turn(raw, cosine, sine).astype(jnp.bfloat16)
        start = start + heads


def join_kernel(*refs):
    *parts, out_ref = refs
    start = 0
    for part in parts:
        out_ref[start : start + part.shape[0]] = part[...]
        start += part.shape[0]


def touch_kernel(seen_ref, in_ref, out_ref):
    out_ref[...] = in_ref[...]


def queries(refs):
    tiles = [ref[:, g * HD : (g + 1) * HD] for ref in refs for g in range(ref.shape[1] // HD)]
    return jnp.concatenate(tiles, axis=0)


def scores_of(keys, query):
    return lax.dot_general(keys, query, (((1,), (1,)), ((), ())), preferred_element_type=jnp.float32)


def weighted(values, weights):
    return lax.dot_general(values, weights, (((0,), (0,)), ((), ())), preferred_element_type=jnp.float32)


def careful(q_sides, kv_refs, states, spare, bases=None):
    gap = lax.broadcasted_iota(jnp.int32, (ROWS, HD), 1) - lax.broadcasted_iota(jnp.int32, (ROWS, HD), 0)
    q_ref, kv_ref = spare
    start = 0
    for ref in kv_refs:
        kv_ref[start : start + ref.shape[0]] = ref[...]
        start += ref.shape[0]
    for q_refs, (top_ref, total_ref, acc_ref) in zip(q_sides, states):
        start = 0
        for ref in q_refs:
            q_ref[:, start : start + ref.shape[1]] = ref[...]
            start += ref.shape[1]

        def body(i, carry, top_ref=top_ref, total_ref=total_ref, acc_ref=acc_ref):
            j, g = i // GROUP, i % GROUP
            rows = pl.ds(pl.multiple_of(j * ROWS, ROWS), ROWS)
            cols = pl.ds(pl.multiple_of(g * HD, HD), HD)
            scores = scores_of(kv_ref[rows, :HD], q_ref[:, cols])
            if bases is not None:
                scores = jnp.where(gap >= bases[j] - bases[SLAB // ROWS], scores, floor_value)
            old = top_ref[:, cols]
            top = jnp.maximum(old, jnp.max(scores, axis=0, keepdims=True) * FACTOR)
            expo = jnp.exp2(scores * FACTOR - top[:1])
            shrink = jnp.exp2(old - top)
            top_ref[:, cols] = top
            total_ref[:, cols] = total_ref[:, cols] * shrink + jnp.sum(expo.reshape(ROWS // 8, 8, HD), axis=0)
            acc_ref[:, cols] = acc_ref[:, cols] * shrink[:1] + weighted(kv_ref[rows, HD:], expo.astype(jnp.bfloat16))
            return carry

        lax.fori_loop(0, SLAB // ROWS * GROUP, body, 0)


def first_kernel(diagonal, base_ref, *refs):
    *q_refs, a_ref, b_ref, top_ref, total_ref, acc_ref, spare_q, spare_kv = refs
    kv = jnp.concatenate([a_ref[...], b_ref[...]], axis=0)
    scores = scores_of(kv[:, :HD], queries(q_refs))
    gap = lax.broadcasted_iota(jnp.int32, (ROWS, HD), 1) - lax.broadcasted_iota(jnp.int32, (ROWS, HD), 0)
    lines = [scores[j * ROWS : (j + 1) * ROWS] for j in range(SLAB // ROWS)]
    seen = jnp.concatenate([gap >= 0] * GROUP, axis=1)
    lines[diagonal] = jnp.where(seen, lines[diagonal], floor_value)
    top = jnp.max(lines[diagonal], axis=0, keepdims=True) * FACTOR
    top = jnp.broadcast_to(top, (8, SIDE))
    parts = []
    for j, line in enumerate(lines):
        hidden = jnp.where(base_ref[j] > base_ref[SLAB // ROWS], -floor_value, 0.0)
        parts.append(jnp.exp2(line.reshape(ROWS // 8, 8, SIDE) * FACTOR - (top + hidden)[None]))
    expo = jnp.concatenate(parts, axis=0)
    total = jnp.sum(expo, axis=0)
    top_ref[...] = top
    total_ref[...] = total
    acc_ref[...] = weighted(kv[:, HD:], expo.astype(jnp.bfloat16).reshape(SLAB, SIDE))

    @pl.when(jnp.logical_not(jnp.max(total) <= ROOM))
    def _():
        total_ref[...] = jnp.zeros_like(total_ref)
        acc_ref[...] = jnp.zeros_like(acc_ref)
        careful([q_refs], (a_ref, b_ref), [(top_ref, total_ref, acc_ref)], (spare_q, spare_kv), base_ref)


def part_of(query, kv, top):
    keys, cols = kv.shape[0], query.shape[0]
    scores = scores_of(kv[:, :HD], query).reshape(keys // 8, 8, cols)
    expo = jnp.exp2(scores * FACTOR - top[None])
    total = jnp.sum(expo, axis=0)
    acc = weighted(kv[:, HD:], expo.astype(jnp.bfloat16).reshape(keys, cols))
    return total, acc, jnp.max(total) <= ROOM


def next_kernel(flag_ref, *refs):
    q_refs, kv_ref, ins, outs, spare, part_ref = refs[:2], refs[2], refs[3:9], refs[9:15], refs[15:17], refs[17]

    @pl.when(flag_ref[0] == 0)
    def _():
        for ref, given in zip(outs, ins):
            ref[...] = given[...]

    @pl.when(flag_ref[0] != 0)
    def _():
        top = jnp.concatenate([ins[0][...], ins[3][...]], axis=1)
        total, part_ref[...], room = part_of(queries(q_refs), kv_ref[...], top)

        @pl.when(room)
        def _():
            for side in range(2):
                cols = slice(side * SIDE, (side + 1) * SIDE)
                outs[3 * side][...] = ins[3 * side][...]
                outs[3 * side + 1][...] = ins[3 * side + 1][...] + total[:, cols]
                outs[3 * side + 2][...] = ins[3 * side + 2][...] + part_ref[:, cols]

        @pl.when(jnp.logical_not(room))
        def _():
            for ref, given in zip(outs, ins):
                ref[...] = given[...]
            careful([q_refs[:1], q_refs[1:]], (kv_ref,), [outs[:3], outs[3:]], spare)


def last_kernel(flag_ref, *refs):
    *q_refs, a_ref, b_ref, top_ref, total_ref, acc_ref, out_ref, spare_q, spare_kv, last_top, last_total, last_acc = refs
    last_total[...] = total_ref[...]
    last_acc[...] = acc_ref[...]

    @pl.when(flag_ref[0] != 0)
    def _():
        kv = jnp.concatenate([a_ref[...], b_ref[...]], axis=0)
        total, acc, room = part_of(queries(q_refs), kv, top_ref[...])
        last_total[...] = total_ref[...] + total
        last_acc[...] = acc_ref[...] + acc

        @pl.when(jnp.logical_not(room))
        def _():
            last_top[...] = top_ref[...]
            last_total[...] = total_ref[...]
            last_acc[...] = acc_ref[...]
            careful([q_refs], (a_ref, b_ref), [(last_top, last_total, last_acc)], (spare_q, spare_kv))

    scale = 1.0 / jnp.sum(last_total[...], axis=0, keepdims=True)
    for g in range(GROUP):
        cols = slice(g * HD, (g + 1) * HD)
        out_ref[:, cols] = (last_acc[:, cols] * scale[:, cols]).T.astype(jnp.bfloat16)


def whole():
    return pl.BlockSpec(memory_space=pltpu.VMEM)


def call(kernel, n_in, outs, n_scalar=1, aliases=None, scratch=(), flops=1 << 16):
    return pl.pallas_call(
        kernel,
        out_shape=outs,
        in_specs=[pl.BlockSpec(memory_space=pltpu.SMEM)] * n_scalar + [whole()] * n_in,
        out_specs=tuple(whole() for _ in outs),
        input_output_aliases=aliases or {},
        scratch_shapes=list(scratch),
        compiler_params=pltpu.CompilerParams(vmem_limit_bytes=VMEM_LIMIT),
        cost_estimate=pl.CostEstimate(flops=flops, bytes_accessed=flops >> 8, transcendentals=0),
    )


def after(array, *others):
    return lax.optimization_barrier((array,) + others)


def touch(seen, array, flops=1 << 34):
    out = jax.ShapeDtypeStruct(array.shape, array.dtype)
    return call(touch_kernel, 2, (out,), 0, {1: 0}, flops=flops)(seen, array)[0]


def place_kernel(group_ref, part_ref, *refs):
    out_hbm, sem = refs[-2:]
    width = part_ref.shape[1]
    columns = pl.ds(pl.multiple_of(group_ref[0] * width, width), width)
    copy = pltpu.make_async_copy(part_ref, out_hbm.at[:, columns], sem)
    copy.start()
    copy.wait()


def place(group, part, *out):
    rows, width = part.shape
    return pl.pallas_call(
        place_kernel,
        out_shape=jax.ShapeDtypeStruct((rows, 2 * width), part.dtype),
        in_specs=[pl.BlockSpec(memory_space=pltpu.SMEM), whole()] + [pl.BlockSpec(memory_space=pl.ANY)] * len(out),
        out_specs=pl.BlockSpec(memory_space=pl.ANY),
        scratch_shapes=[pltpu.SemaphoreType.DMA],
        input_output_aliases={2: 0} if out else {},
        cost_estimate=pl.CostEstimate(flops=1 << 16, bytes_accessed=1 << 18, transcendentals=0),
    )(group.reshape(1), part, *out)


def on_device(activations, adapter_down, adapter_ids, adapter_weight, query_base, key_base, value_base, up_query, up_key, up_value):
    ctx = lax.axis_index("ctx").astype(jnp.int32)
    z, x, core = ctx // (2 * XS), (ctx // 2) % XS, ctx % 2
    group = ((x + 1) // 2) % 2
    groups = group.reshape(1)
    f32, b16 = jnp.float32, jnp.bfloat16
    shape = jax.ShapeDtypeStruct

    low, sent = low_product(activations, adapter_down)

    def pair_up(array, step):
        return send(array, lambda z, x, c, y: (z, x, c, y ^ (1 if c == step else 3)))

    one = pair_up(sent, 0)

    labels = jnp.arange(SPAN, dtype=jnp.int32) // RANK
    coef = jnp.zeros((ROWS, SPAN), f32)
    for j in range(adapter_ids.shape[1]):
        coef = coef + jnp.where(adapter_ids[:, j : j + 1] == labels[None, :], adapter_weight[:, j : j + 1], 0.0)
    positions = (ctx * ROWS + jnp.arange(ROWS, dtype=jnp.int32)).astype(f32)
    inverse = jnp.exp(jnp.arange(HD // 2, dtype=f32) * (-2.0 * math.log(rope_base) / HD))
    angles = positions[:, None] * jnp.concatenate([inverse, inverse])[None, :]
    cosine = jnp.cos(angles)
    sign = jnp.where(jnp.arange(HD) < HD // 2, -1.0, 1.0).astype(f32)
    sine = jnp.sin(angles) * sign[None, :]
    low = call(join_kernel, 1, (shape(low.shape, f32),), 0)(low)[0]
    one, low, coef, cosine, sine = after(one, low, coef, cosine, sine)
    low, sent = call(add_kernel, 2, (shape(low.shape, f32), shape(low.shape, b16)), 0)(low, one)
    two = pair_up(sent, 1)

    kv_shape = shape((ROWS, 2 * HD), b16)
    kv, kv_other, gated_query = call(kv_kernel, 9, (kv_shape, kv_shape, shape((ROWS, SPAN), b16)))(
        groups, low, two, coef, up_key, up_value, key_base, value_base, cosine, sine
    )

    def neighbour(array):
        return send(array, lambda z, x, c, y: (z, x ^ 1, c, y))

    from_3 = send(kv, lambda z, x, c, y: (z, x ^ 3, c, y))
    from_1 = neighbour(kv_other)
    from_2 = send(kv_other, lambda z, x, c, y: (z, x ^ 2, c, y))
    side_shape = shape((ROWS, GROUP * HD), b16)
    q_own, q_other = call(q_kernel, 5, (side_shape, side_shape))(
        groups, gated_query, up_query, query_base, cosine, sine
    )
    q_rest = neighbour(q_other)
    q_own = touch(q_other, q_own, 1 << 36)
    from_1, from_2, from_3, q_own = after(from_1, from_2, from_3, q_own)

    def join(*parts):
        rows = sum(part.shape[0] for part in parts)
        return call(join_kernel, len(parts), (shape((rows, 2 * HD), b16),), 0)(*parts)[0]

    moving_a = join(kv, from_1, from_3, from_2)

    def ring(array):
        return send(array, lambda z, x, c, y: (z + (1 if c == 0 else -1), x, c, y))

    arriving_a = ring(moving_a)
    moving_b = swap_cores(moving_a)
    arriving_b = ring(moving_b)
    q_own = touch(moving_b, q_own, 1 << 30)

    blocks = (jnp.stack([x, x ^ 1, x ^ 3, x ^ 2]) - x) * BLOCK
    keys_at = jnp.concatenate([blocks + core * ROWS, blocks + (1 - core) * ROWS])

    def bases(start):
        return jnp.concatenate([keys_at, start.reshape(1)]).astype(jnp.int32)

    spare = [pltpu.VMEM((ROWS, SIDE), b16), pltpu.VMEM((SLAB, 2 * HD), b16)]
    state_shape = (shape((8, SIDE), f32), shape((8, SIDE), f32), shape((HD, SIDE), f32))
    state = [
        *call(functools.partial(first_kernel, 0), 3, state_shape, scratch=spare)(bases(core * ROWS), q_own, moving_a, moving_b),
    ]
    q_rest, *state = after(q_rest, *state)
    state += call(functools.partial(first_kernel, 1), 3, state_shape, scratch=spare)(
        bases(((x ^ 1) - x) * BLOCK + core * ROWS), q_rest, moving_a, moving_b
    )

    def attend(flag, kv, state):
        aliases = {4 + k: k for k in range(6)}
        scratch = [*spare, pltpu.VMEM((HD, 2 * SIDE), f32)]
        return call(next_kernel, 9, state_shape * 2, 1, aliases, scratch)(
            flag.astype(jnp.int32).reshape(1), q_own, q_rest, kv, *state
        )

    def take(arriving, state, onward=ring, flops=1 << 34):
        arrived, *state = after(arriving, *state)
        if onward is None:
            return arrived, None, state
        arriving = onward(arrived)
        return arrived, arriving, [touch(arrived, state[0], flops), *state[1:]]

    moving_a, arriving_a, state = take(arriving_a, state, flops=1 << 31)
    for step in range(1, 4):
        below, wrapped = z >= step, z + step >= ZS
        moving_b, arriving_b, state = take(arriving_b, state, ring if step < 3 else None)
        moving = join(moving_a, moving_b)
        swapped = swap_cores(moving)
        state = attend(jnp.where(core == 0, below, wrapped), moving, state)
        moving_a, arriving_a, state = take(arriving_a, state, ring if step < 3 else swap_cores)
        state = attend(jnp.where(core == 0, wrapped, below), swapped, state)
    moving_b, *state = after(arriving_a, *state)
    flag = (z >= ZS // 2).astype(jnp.int32).reshape(1)

    def finish(query, state):
        scratch = spare + [pltpu.VMEM((8, SIDE), f32)] * 2 + [pltpu.VMEM((HD, SIDE), f32)]
        return call(last_kernel, 6, (side_shape,), scratch=scratch)(
            flag, query, moving_a, moving_b, *state
        )[0]

    back = neighbour(finish(q_rest, state[3:]))
    own = finish(q_own, state[:3])
    out = place(group, own)
    back, out = after(back, out)
    return place(1 - group, back, out)


def solution(mesh):
    in_specs = (
        P("ctx", "head"),
        P("head", None),
        P("ctx", None),
        P("ctx", None),
        P("ctx", "head"),
        P("ctx", "head"),
        P("ctx", "head"),
        P(None, "head"),
        P(None, "head"),
        P(None, "head"),
    )
    return jax.shard_map(on_device, mesh=mesh, in_specs=in_specs, out_specs=P("ctx", "head"), check_vma=False)
```

```python
import functools
import math

import jax
import jax.numpy as jnp
from jax import lax
from jax.experimental import pallas as pl
from jax.experimental.pallas import tpu as pltpu
from jax.sharding import PartitionSpec as P

HD = 128
ADAPTERS = 8
RANK = 32
SPAN = ADAPTERS * RANK
ROWS = 128
GROUP = 8
ZS, XS, YS = 8, 4, 4
BLOCK = 2 * ROWS
SLAB = XS * BLOCK
SIDE = GROUP * ROWS

rope_base = 500000.0
floor_value = -1e30
FACTOR = math.log2(math.e) / math.sqrt(HD)
ROOM = 2.0**60
VMEM_LIMIT = 40 * 1024 * 1024


def device(z, x, core, y):
    return (((z % ZS) * XS + x % XS) * 2 + core) * YS + y


def send(array, move):
    pairs = []
    for z in range(ZS):
        for x in range(XS):
            for core in range(2):
                for y in range(YS):
                    pairs.append((device(z, x, core, y), device(*move(z, x, core, y))))
    return lax.ppermute(array, ("ctx", "head"), pairs)


def swap_cores(array):
    return send(array, lambda z, x, core, y: (z, x, 1 - core, y))


def turn(raw, cosine, sine):
    return raw * cosine + pltpu.roll(raw, HD // 2, 1) * sine


def low_kernel(act_hbm, down_hbm, low_ref, sent_ref, act_ref, down_ref, act_sem, down_sem):
    pieces = act_sem.shape[0]
    depth = act_ref.shape[1] // pieces
    copies = []
    for k in range(pieces):
        span = slice(k * depth, (k + 1) * depth)
        copies.append(
            (
                pltpu.make_async_copy(act_hbm.at[:, span], act_ref.at[:, span], act_sem.at[k]),
                pltpu.make_async_copy(down_hbm.at[span], down_ref.at[span], down_sem.at[k]),
            )
        )
        for copy in copies[-1]:
            copy.start()
    total = None
    for k in range(pieces):
        span = slice(k * depth, (k + 1) * depth)
        for copy in copies[k]:
            copy.wait()
        part = jnp.dot(act_ref[:, span], down_ref[span], preferred_element_type=jnp.float32)
        total = part if total is None else total + part
    low_ref[...] = total
    sent_ref[...] = total.astype(jnp.bfloat16)


def low_product(activations, adapter_down):
    rows, columns = activations.shape[0], adapter_down.shape[1]
    pieces = 4
    return pl.pallas_call(
        low_kernel,
        in_specs=[pl.BlockSpec(memory_space=pltpu.HBM)] * 2,
        out_specs=(whole(), whole()),
        out_shape=(
            jax.ShapeDtypeStruct((rows, columns), jnp.float32),
            jax.ShapeDtypeStruct((rows, columns), jnp.bfloat16),
        ),
        scratch_shapes=[
            pltpu.VMEM(activations.shape, activations.dtype),
            pltpu.VMEM(adapter_down.shape, adapter_down.dtype),
            pltpu.SemaphoreType.DMA((pieces,)),
            pltpu.SemaphoreType.DMA((pieces,)),
        ],
        compiler_params=pltpu.CompilerParams(vmem_limit_bytes=56 * 1024 * 1024),
        cost_estimate=pl.CostEstimate(flops=1 << 29, bytes_accessed=4 << 20, transcendentals=0),
    )(activations, adapter_down)


def add_kernel(low_ref, got_ref, sum_ref, sent_ref):
    total = low_ref[...] + got_ref[...].astype(jnp.float32)
    sum_ref[...] = total
    sent_ref[...] = total.astype(jnp.bfloat16)


def gated(low, more, coef):
    return ((low + more.astype(jnp.float32)) * coef).astype(jnp.bfloat16)


def kv_kernel(group_ref, low_ref, more_ref, coef_ref, upk_ref, upv_ref, kb_ref, vb_ref, cos_ref, sin_ref, mine_ref, other_ref, gq_ref):
    group = group_ref[0]
    coef = coef_ref[...]
    gq_ref[...], gk, gv = [
        gated(low_ref[:, p * SPAN : (p + 1) * SPAN], more_ref[:, p * SPAN : (p + 1) * SPAN], coef) for p in range(3)
    ]
    key_raw = kb_ref[...].astype(jnp.float32) + jnp.dot(gk, upk_ref[...], preferred_element_type=jnp.float32)
    value = vb_ref[...].astype(jnp.float32) + jnp.dot(gv, upv_ref[...], preferred_element_type=jnp.float32)
    cosine, sine = cos_ref[...], sin_ref[...]
    keys = [turn(key_raw[:, h * HD : (h + 1) * HD], cosine, sine) for h in range(2)]
    values = [value[:, h * HD : (h + 1) * HD] for h in range(2)]
    first = group == 0
    mine_ref[:, :HD] = jnp.where(first, keys[0], keys[1]).astype(jnp.bfloat16)
    mine_ref[:, HD:] = jnp.where(first, values[0], values[1]).astype(jnp.bfloat16)
    other_ref[:, :HD] = jnp.where(first, keys[1], keys[0]).astype(jnp.bfloat16)
    other_ref[:, HD:] = jnp.where(first, values[1], values[0]).astype(jnp.bfloat16)


def q_kernel(group_ref, gq_ref, upq_ref, qb_ref, cos_ref, sin_ref, mine_ref, *other_refs):
    own = group_ref[0]
    cosine, sine = cos_ref[...], sin_ref[...]
    gq = gq_ref[...]
    start = (1 - own) * GROUP
    for target in (*other_refs, mine_ref):
        heads = target.shape[1] // HD
        if target is mine_ref:
            start = own * GROUP
        for j in range(heads):
            cols = pl.ds(pl.multiple_of((start + j) * HD, HD), HD)
            raw = qb_ref[:, cols].astype(jnp.float32) + jnp.dot(
                gq, upq_ref[:, cols], preferred_element_type=jnp.float32
            )
            target[:, j * HD : (j + 1) * HD] = turn(raw, cosine, sine).astype(jnp.bfloat16)
        start = start + heads


def join_kernel(*refs):
    *parts, out_ref = refs
    start = 0
    for part in parts:
        out_ref[start : start + part.shape[0]] = part[...]
        start += part.shape[0]


def touch_kernel(seen_ref, in_ref, out_ref):
    out_ref[...] = in_ref[...]


def queries(refs):
    tiles = [ref[:, g * HD : (g + 1) * HD] for ref in refs for g in range(ref.shape[1] // HD)]
    return jnp.concatenate(tiles, axis=0)


def scores_of(keys, query):
    return lax.dot_general(keys, query, (((1,), (1,)), ((), ())), preferred_element_type=jnp.float32)


def weighted(values, weights):
    return lax.dot_general(values, weights, (((0,), (0,)), ((), ())), preferred_element_type=jnp.float32)


def careful(q_sides, kv_refs, states, spare, bases=None):
    gap = lax.broadcasted_iota(jnp.int32, (ROWS, HD), 1) - lax.broadcasted_iota(jnp.int32, (ROWS, HD), 0)
    q_ref, kv_ref = spare
    start = 0
    for ref in kv_refs:
        kv_ref[start : start + ref.shape[0]] = ref[...]
        start += ref.shape[0]
    for q_refs, (top_ref, total_ref, acc_ref) in zip(q_sides, states):
        start = 0
        for ref in q_refs:
            q_ref[:, start : start + ref.shape[1]] = ref[...]
            start += ref.shape[1]

        def body(i, carry, top_ref=top_ref, total_ref=total_ref, acc_ref=acc_ref):
            j, g = i // GROUP, i % GROUP
            rows = pl.ds(pl.multiple_of(j * ROWS, ROWS), ROWS)
            cols = pl.ds(pl.multiple_of(g * HD, HD), HD)
            scores = scores_of(kv_ref[rows, :HD], q_ref[:, cols])
            if bases is not None:
                scores = jnp.where(gap >= bases[j] - bases[SLAB // ROWS], scores, floor_value)
            old = top_ref[:, cols]
            top = jnp.maximum(old, jnp.max(scores, axis=0, keepdims=True) * FACTOR)
            expo = jnp.exp2(scores * FACTOR - top[:1])
            shrink = jnp.exp2(old - top)
            top_ref[:, cols] = top
            total_ref[:, cols] = total_ref[:, cols] * shrink + jnp.sum(expo.reshape(ROWS // 8, 8, HD), axis=0)
            acc_ref[:, cols] = acc_ref[:, cols] * shrink[:1] + weighted(kv_ref[rows, HD:], expo.astype(jnp.bfloat16))
            return carry

        lax.fori_loop(0, SLAB // ROWS * GROUP, body, 0)


def first_kernel(diagonal, base_ref, *refs):
    *q_refs, a_ref, b_ref, top_ref, total_ref, acc_ref, spare_q, spare_kv = refs
    kv = jnp.concatenate([a_ref[...], b_ref[...]], axis=0)
    scores = scores_of(kv[:, :HD], queries(q_refs))
    gap = lax.broadcasted_iota(jnp.int32, (ROWS, HD), 1) - lax.broadcasted_iota(jnp.int32, (ROWS, HD), 0)
    lines = [scores[j * ROWS : (j + 1) * ROWS] for j in range(SLAB // ROWS)]
    seen = jnp.concatenate([gap >= 0] * GROUP, axis=1)
    lines[diagonal] = jnp.where(seen, lines[diagonal], floor_value)
    top = jnp.max(lines[diagonal], axis=0, keepdims=True) * FACTOR
    top = jnp.broadcast_to(top, (8, SIDE))
    parts = []
    for j, line in enumerate(lines):
        hidden = jnp.where(base_ref[j] > base_ref[SLAB // ROWS], -floor_value, 0.0)
        parts.append(jnp.exp2(line.reshape(ROWS // 8, 8, SIDE) * FACTOR - (top + hidden)[None]))
    expo = jnp.concatenate(parts, axis=0)
    total = jnp.sum(expo, axis=0)
    top_ref[...] = top
    total_ref[...] = total
    acc_ref[...] = weighted(kv[:, HD:], expo.astype(jnp.bfloat16).reshape(SLAB, SIDE))

    @pl.when(jnp.logical_not(jnp.max(total) <= ROOM))
    def _():
        total_ref[...] = jnp.zeros_like(total_ref)
        acc_ref[...] = jnp.zeros_like(acc_ref)
        careful([q_refs], (a_ref, b_ref), [(top_ref, total_ref, acc_ref)], (spare_q, spare_kv), base_ref)


def part_of(query, kv, top):
    keys, cols = kv.shape[0], query.shape[0]
    scores = scores_of(kv[:, :HD], query).reshape(keys // 8, 8, cols)
    expo = jnp.exp2(scores * FACTOR - top[None])
    total = jnp.sum(expo, axis=0)
    acc = weighted(kv[:, HD:], expo.astype(jnp.bfloat16).reshape(keys, cols))
    return total, acc, jnp.max(total) <= ROOM


def next_kernel(flag_ref, *refs):
    q_refs, kv_ref, ins, outs, spare, part_ref = refs[:2], refs[2], refs[3:9], refs[9:15], refs[15:17], refs[17]

    @pl.when(flag_ref[0] == 0)
    def _():
        for ref, given in zip(outs, ins):
            ref[...] = given[...]

    @pl.when(flag_ref[0] != 0)
    def _():
        top = jnp.concatenate([ins[0][...], ins[3][...]], axis=1)
        total, part_ref[...], room = part_of(queries(q_refs), kv_ref[...], top)

        @pl.when(room)
        def _():
            for side in range(2):
                cols = slice(side * SIDE, (side + 1) * SIDE)
                outs[3 * side][...] = ins[3 * side][...]
                outs[3 * side + 1][...] = ins[3 * side + 1][...] + total[:, cols]
                outs[3 * side + 2][...] = ins[3 * side + 2][...] + part_ref[:, cols]

        @pl.when(jnp.logical_not(room))
        def _():
            for ref, given in zip(outs, ins):
                ref[...] = given[...]
            careful([q_refs[:1], q_refs[1:]], (kv_ref,), [outs[:3], outs[3:]], spare)


def last_kernel(flag_ref, *refs):
    *q_refs, a_ref, b_ref, top_ref, total_ref, acc_ref, out_ref, spare_q, spare_kv, last_top, last_total, last_acc = refs
    last_total[...] = total_ref[...]
    last_acc[...] = acc_ref[...]

    @pl.when(flag_ref[0] != 0)
    def _():
        kv = jnp.concatenate([a_ref[...], b_ref[...]], axis=0)
        total, acc, room = part_of(queries(q_refs), kv, top_ref[...])
        last_total[...] = total_ref[...] + total
        last_acc[...] = acc_ref[...] + acc

        @pl.when(jnp.logical_not(room))
        def _():
            last_top[...] = top_ref[...]
            last_total[...] = total_ref[...]
            last_acc[...] = acc_ref[...]
            careful([q_refs], (a_ref, b_ref), [(last_top, last_total, last_acc)], (spare_q, spare_kv))

    scale = 1.0 / jnp.sum(last_total[...], axis=0, keepdims=True)
    for g in range(GROUP):
        cols = slice(g * HD, (g + 1) * HD)
        out_ref[:, cols] = (last_acc[:, cols] * scale[:, cols]).T.astype(jnp.bfloat16)


def whole():
    return pl.BlockSpec(memory_space=pltpu.VMEM)


def call(kernel, n_in, outs, n_scalar=1, aliases=None, scratch=(), flops=1 << 16):
    return pl.pallas_call(
        kernel,
        out_shape=outs,
        in_specs=[pl.BlockSpec(memory_space=pltpu.SMEM)] * n_scalar + [whole()] * n_in,
        out_specs=tuple(whole() for _ in outs),
        input_output_aliases=aliases or {},
        scratch_shapes=list(scratch),
        compiler_params=pltpu.CompilerParams(vmem_limit_bytes=VMEM_LIMIT),
        cost_estimate=pl.CostEstimate(flops=flops, bytes_accessed=flops >> 8, transcendentals=0),
    )


def after(array, *others):
    return lax.optimization_barrier((array,) + others)


def touch(seen, array, flops=1 << 34):
    out = jax.ShapeDtypeStruct(array.shape, array.dtype)
    return call(touch_kernel, 2, (out,), 0, {1: 0}, flops=flops)(seen, array)[0]


def on_device(activations, adapter_down, adapter_ids, adapter_weight, query_base, key_base, value_base, up_query, up_key, up_value):
    ctx = lax.axis_index("ctx").astype(jnp.int32)
    z, x, core = ctx // (2 * XS), (ctx // 2) % XS, ctx % 2
    group = ((x + 1) // 2) % 2
    groups = group.reshape(1)
    f32, b16 = jnp.float32, jnp.bfloat16
    shape = jax.ShapeDtypeStruct

    low, sent = low_product(activations, adapter_down)

    def pair_up(array, step):
        return send(array, lambda z, x, c, y: (z, x, c, y ^ (1 if c == step else 3)))

    one = pair_up(sent, 0)

    labels = jnp.arange(SPAN, dtype=jnp.int32) // RANK
    coef = jnp.zeros((ROWS, SPAN), f32)
    for j in range(adapter_ids.shape[1]):
        coef = coef + jnp.where(adapter_ids[:, j : j + 1] == labels[None, :], adapter_weight[:, j : j + 1], 0.0)
    positions = (ctx * ROWS + jnp.arange(ROWS, dtype=jnp.int32)).astype(f32)
    inverse = jnp.exp(jnp.arange(HD // 2, dtype=f32) * (-2.0 * math.log(rope_base) / HD))
    angles = positions[:, None] * jnp.concatenate([inverse, inverse])[None, :]
    cosine = jnp.cos(angles)
    sign = jnp.where(jnp.arange(HD) < HD // 2, -1.0, 1.0).astype(f32)
    sine = jnp.sin(angles) * sign[None, :]
    low = call(join_kernel, 1, (shape(low.shape, f32),), 0)(low)[0]
    one, low, coef, cosine, sine = after(one, low, coef, cosine, sine)
    low, sent = call(add_kernel, 2, (shape(low.shape, f32), shape(low.shape, b16)), 0)(low, one)
    two = pair_up(sent, 1)

    kv_shape = shape((ROWS, 2 * HD), b16)
    kv, kv_other, gated_query = call(kv_kernel, 9, (kv_shape, kv_shape, shape((ROWS, SPAN), b16)))(
        groups, low, two, coef, up_key, up_value, key_base, value_base, cosine, sine
    )

    def neighbour(array):
        return send(array, lambda z, x, c, y: (z, x ^ 1, c, y))

    from_3 = send(kv, lambda z, x, c, y: (z, x ^ 3, c, y))
    from_1 = neighbour(kv_other)
    from_2 = send(kv_other, lambda z, x, c, y: (z, x ^ 2, c, y))
    side_shape = shape((ROWS, GROUP * HD), b16)
    q_own, q_other = call(q_kernel, 5, (side_shape, side_shape))(
        groups, gated_query, up_query, query_base, cosine, sine
    )
    q_rest = neighbour(q_other)
    q_own = touch(q_other, q_own, 1 << 36)
    from_1, from_2, from_3, q_own = after(from_1, from_2, from_3, q_own)

    def join(*parts):
        rows = sum(part.shape[0] for part in parts)
        return call(join_kernel, len(parts), (shape((rows, 2 * HD), b16),), 0)(*parts)[0]

    moving_a = join(kv, from_1, from_3, from_2)

    def ring(array):
        return send(array, lambda z, x, c, y: (z + (1 if c == 0 else -1), x, c, y))

    arriving_a = ring(moving_a)
    moving_b = swap_cores(moving_a)
    arriving_b = ring(moving_b)
    q_own = touch(moving_b, q_own, 1 << 30)

    blocks = (jnp.stack([x, x ^ 1, x ^ 3, x ^ 2]) - x) * BLOCK
    keys_at = jnp.concatenate([blocks + core * ROWS, blocks + (1 - core) * ROWS])

    def bases(start):
        return jnp.concatenate([keys_at, start.reshape(1)]).astype(jnp.int32)

    spare = [pltpu.VMEM((ROWS, SIDE), b16), pltpu.VMEM((SLAB, 2 * HD), b16)]
    state_shape = (shape((8, SIDE), f32), shape((8, SIDE), f32), shape((HD, SIDE), f32))
    state = [
        *call(functools.partial(first_kernel, 0), 3, state_shape, scratch=spare)(bases(core * ROWS), q_own, moving_a, moving_b),
    ]
    q_rest, *state = after(q_rest, *state)
    state += call(functools.partial(first_kernel, 1), 3, state_shape, scratch=spare)(
        bases(((x ^ 1) - x) * BLOCK + core * ROWS), q_rest, moving_a, moving_b
    )

    def attend(flag, kv, state):
        aliases = {4 + k: k for k in range(6)}
        scratch = [*spare, pltpu.VMEM((HD, 2 * SIDE), f32)]
        return call(next_kernel, 9, state_shape * 2, 1, aliases, scratch)(
            flag.astype(jnp.int32).reshape(1), q_own, q_rest, kv, *state
        )

    def take(arriving, state, onward=ring, flops=1 << 34):
        arrived, *state = after(arriving, *state)
        if onward is None:
            return arrived, None, state
        arriving = onward(arrived)
        return arrived, arriving, [touch(arrived, state[0], flops), *state[1:]]

    moving_a, arriving_a, state = take(arriving_a, state, flops=1 << 31)
    for step in range(1, 4):
        below, wrapped = z >= step, z + step >= ZS
        moving_b, arriving_b, state = take(arriving_b, state, ring if step < 3 else None)
        moving = join(moving_a, moving_b)
        swapped = swap_cores(moving)
        state = attend(jnp.where(core == 0, below, wrapped), moving, state)
        moving_a, arriving_a, state = take(arriving_a, state, ring if step < 3 else swap_cores)
        state = attend(jnp.where(core == 0, wrapped, below), swapped, state)
    moving_b, *state = after(arriving_a, *state)
    flag = (z >= ZS // 2).astype(jnp.int32).reshape(1)

    def finish(query, state):
        scratch = spare + [pltpu.VMEM((8, SIDE), f32)] * 2 + [pltpu.VMEM((HD, SIDE), f32)]
        return call(last_kernel, 6, (side_shape,), scratch=scratch)(
            flag, query, moving_a, moving_b, *state
        )[0]

    back = neighbour(finish(q_rest, state[3:]))
    own = finish(q_own, state[:3])
    return jnp.concatenate([jnp.where(group == 0, own, back), jnp.where(group == 0, back, own)], axis=1)


def solution(mesh):
    in_specs = (
        P("ctx", "head"),
        P("head", None),
        P("ctx", None),
        P("ctx", None),
        P("ctx", "head"),
        P("ctx", "head"),
        P("ctx", "head"),
        P(None, "head"),
        P(None, "head"),
        P(None, "head"),
    )
    return jax.shard_map(on_device, mesh=mesh, in_specs=in_specs, out_specs=P("ctx", "head"), check_vma=False)
```
